256 devices in a mesh: energy: 64 (over z, x, core), slab: 4 (over y).
Axes of the slice: x: 4, y: 4, z: 8, core: 2. Of those that a mesh axis runs over, the one named last changes fastest.
Arguments:
- green: bfloat16 [2048, 36864], P('energy', 'slab'), may hold values from -1.75 to 1.75
- sigma_in: bfloat16 [2048, 36864], P('energy', 'slab'), may hold values from -6 to 6
- neighbours: int32 [256, 8], P('slab'), may hold values from 0 to 95
- coupling: float32 [256, 8], P('slab'), may hold values from 0.1 to 1
- send_down: int32 [4, 16], P('slab'), may hold values from 0 to 63, as said below
- send_up: int32 [4, 16], P('slab'), may hold values from 0 to 63, as said below
- offsets: int32 [16], replicated, may hold values from 1 to 32, as said below
- w_emit: float32 [16], replicated, may hold values from 0.02 to 0.2
- w_absorb: float32 [16], replicated, may hold values from 0.02 to 0.2
Outputs:
- sigma_ph: bfloat16 [2048, 36864], P('energy', 'slab')
- g_less: bfloat16 [2048, 36864], P('energy', 'slab')
The draws below stay inside these ranges and needn't reach their ends.
Inputs may be any that keep to these rules, and one draw needn't show every extreme that they name: Each row of send_down holds 16 distinct atom numbers of one slab. Each row of send_up holds 16 distinct atom numbers of one slab. The 16 offsets are distinct, and 32 is one of them.
All inputs are finite; a program needn't handle non-finite values.
Results may differ from the reference program's by a relative error of at most 0.0063.
Values may be sent and summed in bfloat16 or wider, within the bound.
No kernel may reach another device: no remote copies, remote signals or barrier semaphores. Data moves between devices by JAX's collectives and lax.ppermute only.
A program may use at most 128 MiB of HBM per device.

```python
import math
import jax
import jax.numpy as jnp
from jax import lax

ORB = 12
NBRS = 8
FREQS = 16
PAIRS = 144
ENERGIES = 2048
ATOMS_SLAB = 64
SLABS = 4
ATOMS = 256
HB = 16
MAXOFF = 32
N_SLAB = 4


def boundary_lists(key):
    keys = jax.random.split(key, SLABS)
    rows = [jax.random.permutation(keys[number], ATOMS_SLAB)[:HB] for number in range(SLABS)]
    return jnp.stack(rows).astype(jnp.int32)


def draw_send_down(key, part):
    return boundary_lists(jax.random.fold_in(key, 11))


def draw_send_up(key, part):
    return boundary_lists(jax.random.fold_in(key, 23))


def draw_offsets(key, part):
    first, second = jax.random.split(jax.random.fold_in(key, 37))
    chosen = jax.random.permutation(first, MAXOFF - 1)[:FREQS - 1] + 1
    values = jnp.concatenate([chosen.astype(jnp.int32), jnp.array([MAXOFF], jnp.int32)])
    return jax.random.permutation(second, values).astype(jnp.int32)


def plant(drawn, own_key, low, high):
    longest = drawn.shape.index(max(drawn.shape))
    spots = []
    for shift in (0, 1):
        where = [jax.random.randint(jax.random.fold_in(own_key, axis), (), 0, length) for axis, length in enumerate(drawn.shape)]
        where[longest] = (where[longest] + shift) % drawn.shape[longest]
        spots.append(tuple(where))
    return drawn.at[spots[0]].set(low).at[spots[1]].set(high)


def levels(rng, extent, cuts, low, top_value):
    level = 1.0
    for dim, shards_of in cuts:
        steps = jax.random.uniform(jax.random.fold_in(jax.random.fold_in(rng, 6), dim), (shards_of,), jnp.float32, low / len(cuts), top_value / len(cuts))
        level = level * jnp.repeat(jnp.exp(steps), extent[dim] // shards_of).reshape((-1,) + (1,) * (len(extent) - 1 - dim))
    return level


def centred(key, extent, width, limit, shards=(), kind=jnp.bfloat16):
    values = jax.random.normal(key, extent, jnp.float32) * width
    if len(shards) > 0:
        values = levels(key, extent, shards, -0.22, 0.18) * values
    return jnp.clip(values, min=-limit, max=limit).astype(kind)


def setup_inputs(seed: int = 0) -> dict:
    key_list = jax.random.split(jax.random.key(seed), 10)
    return {
        "green": centred(key_list[0], (ENERGIES, ATOMS * PAIRS), ORB ** -0.5, 1.75, ((0, 64), (1, 4))),
        "sigma_in": centred(key_list[1], (ENERGIES, ATOMS * PAIRS), 1.0, 6.0, ((0, 64), (1, 4))),
        "neighbours": plant(jax.random.randint(key_list[2], (ATOMS, NBRS), 0, ATOMS_SLAB + 2 * HB), jax.random.fold_in(key_list[2], 1), 0, (ATOMS_SLAB + 2 * HB) - 1).astype(jnp.int32),
        "coupling": jnp.clip(jnp.exp(math.log(1.0) - 2.3025851 * jax.random.uniform(key_list[3], (ATOMS, NBRS), jnp.float32) ** levels(key_list[3], (ATOMS, NBRS), ((0, 4),), -0.2, 0.2)), 0.1, 1.0),
        "send_down": draw_send_down(jax.random.fold_in(key_list[9], 71), 0),
        "send_up": draw_send_up(jax.random.fold_in(key_list[9], 71), 0),
        "offsets": draw_offsets(jax.random.fold_in(key_list[9], 71), 0),
        "w_emit": jnp.clip(jnp.exp(jax.random.uniform(key_list[7], (FREQS,), jnp.float32, math.log(0.02), math.log(0.2))), 0.02, 0.2),
        "w_absorb": jnp.clip(jnp.exp(jax.random.uniform(key_list[8], (FREQS,), jnp.float32, math.log(0.02), math.log(0.2))), 0.02, 0.2),
    }


def blocks(array):
    return array.astype(jnp.float32).reshape(array.shape[0], array.shape[1], ORB, ORB)


def sandwich(green, middle):
    left_side = blocks(green)
    product = jnp.einsum("eaij,eajk->eaik", left_side, middle, precision=lax.Precision.HIGHEST)
    result = jnp.einsum("eaik,ealk->eail", product, left_side, precision=lax.Precision.HIGHEST)
    return result.reshape(green.shape[0], green.shape[1], ORB * ORB)


def toeplitz(offsets, w_emit, w_absorb, count):
    positions = jnp.arange(count, dtype=jnp.int32)
    distance = positions[:, None] - positions[None, :]
    kernel = jnp.zeros((count, count), jnp.float32)
    for freq in range(offsets.shape[0]):
        kernel = kernel + w_emit[freq] * (distance == offsets[freq]).astype(jnp.float32)
        kernel = kernel + w_absorb[freq] * (distance == -offsets[freq]).astype(jnp.float32)
    return kernel.astype(jnp.bfloat16)


def reference(green, sigma_in, neighbours, coupling, send_down, send_up, offsets, w_emit, w_absorb):
    green = green.reshape(ENERGIES, ATOMS, PAIRS)
    sigma_in = sigma_in.reshape(ENERGIES, ATOMS, PAIRS)
    lesser = sandwich(green, blocks(sigma_in)).astype(jnp.bfloat16)
    kernel = toeplitz(offsets, w_emit, w_absorb, ENERGIES)
    pieces = []
    for slab_index in range(N_SLAB):
        start = slab_index * ATOMS_SLAB
        own = lesser[:, start:start + ATOMS_SLAB]
        if slab_index > 0:
            below = lesser[:, start - ATOMS_SLAB + send_up[slab_index - 1]]
        else:
            below = jnp.zeros((ENERGIES, HB, PAIRS), jnp.bfloat16)
        if slab_index < N_SLAB - 1:
            above = lesser[:, start + ATOMS_SLAB + send_down[slab_index + 1]]
        else:
            above = jnp.zeros((ENERGIES, HB, PAIRS), jnp.bfloat16)
        extended = jnp.concatenate([own, below, above], axis=1)
        total = jnp.zeros((ENERGIES, ATOMS_SLAB, PAIRS), jnp.float32)
        for column in range(NBRS):
            weights = coupling[start:start + ATOMS_SLAB, column]
            picked = extended[:, neighbours[start:start + ATOMS_SLAB, column]]
            total = total + weights[None, :, None] * picked.astype(jnp.float32)
        mixed = total.astype(jnp.bfloat16)
        sigma = jnp.dot(kernel, mixed.reshape(ENERGIES, ATOMS_SLAB * PAIRS), preferred_element_type=jnp.float32)
        pieces.append(sigma.astype(jnp.bfloat16).reshape(ENERGIES, ATOMS_SLAB, PAIRS))
    sigma_ph = jnp.concatenate(pieces, axis=1)
    combined = sigma_in.astype(jnp.float32) + sigma_ph.astype(jnp.float32)
    middle = combined.reshape(ENERGIES, ATOMS, ORB, ORB)
    g_less = sandwich(green, middle).astype(jnp.bfloat16)
    return sigma_ph.reshape(ENERGIES, ATOMS * PAIRS), g_less.reshape(ENERGIES, ATOMS * PAIRS)
```

```python
import jax
import jax.numpy as jnp
from jax import lax
from jax.experimental import pallas as pl
from jax.experimental.pallas import tpu as pltpu
from jax.sharding import PartitionSpec as P

ORB = 12
PAIRS = 144
NBRS = 8
LANES = 128
GROUPS = 4
ROWS = 32
NEAR = 16
SPAN = NEAR * PAIRS
TILES = SPAN // LANES
QUADS = PAIRS // GROUPS
WIDTH = PAIRS * ROWS
F32 = jnp.float32
BF16 = jnp.bfloat16


def lane_iota(shape):
    return lax.broadcasted_iota(jnp.int32, shape, len(shape) - 1)


def row_iota(shape):
    return lax.broadcasted_iota(jnp.int32, shape, len(shape) - 2)


def identity():
    return (lane_iota((LANES, LANES)) == row_iota((LANES, LANES))).astype(BF16)


def flip(eye, tile):
    return lax.dot_general(eye, tile, (((1,), (1,)), ((), ())), preferred_element_type=F32)


def to_batch_lanes(source, flat, target):
    eye = identity()

    for t in range(TILES):
        columns = [source[:, h * SPAN + t * LANES : h * SPAN + (t + 1) * LANES] for h in range(GROUPS)]
        flat[t * LANES : (t + 1) * LANES, :] = flip(eye, jnp.concatenate(columns, axis=0))

    for p in range(PAIRS):
        for g in range(2):
            target[p, 8 * g : 8 * g + 8, :] = flat[pl.ds(8 * g * PAIRS + p, 8, stride=PAIRS), :]


def to_energy_rows(flat, target):
    eye = identity()

    for t in range(TILES):
        turned = flip(eye, flat[t * LANES : (t + 1) * LANES, :].astype(BF16)).astype(BF16)
        for h in range(GROUPS):
            column = h * SPAN + t * LANES
            target[:, column : column + LANES] = turned[h * ROWS : (h + 1) * ROWS]


def sandwich(left, middle, store):
    depth = 3

    def body(step, carry):
        g = step % 2
        first = (step // 2) * depth
        half = pl.ds(pl.multiple_of(g * 8, 8), 8)
        product = [[None] * ORB for _ in range(depth)]
        for j in range(ORB):
            lhs = [left[(first + r) * ORB + j, half, :] for r in range(depth)]
            for k in range(ORB):
                rhs = middle[j * ORB + k, half, :]
                for r in range(depth):
                    term = lhs[r] * rhs
                    product[r][k] = term if j == 0 else product[r][k] + term
        for l in range(ORB):
            total = [None] * depth
            for k in range(ORB):
                rhs = left[l * ORB + k, half, :]
                for r in range(depth):
                    term = product[r][k] * rhs
                    total[r] = term if k == 0 else total[r] + term
            for r in range(depth):
                store((first + r) * ORB + l, g, half, total[r])
        return carry

    lax.fori_loop(0, 2 * ORB // depth, body, 0)


def swap_chunks(values):
    chunk = lane_iota(values[0].shape) // ROWS
    low = chunk % 2 == 0
    out = list(values)
    for a, b in ((0, 1), (2, 3)):
        x, y = out[a], out[b]
        out[a] = jnp.where(low, x, pltpu.roll(y, ROWS, 1))
        out[b] = jnp.where(low, pltpu.roll(x, LANES - ROWS, 1), y)
    low = chunk < 2
    for a, b in ((0, 2), (1, 3)):
        x, y = out[a], out[b]
        out[a] = jnp.where(low, x, pltpu.roll(y, 2 * ROWS, 1))
        out[b] = jnp.where(low, pltpu.roll(x, LANES - 2 * ROWS, 1), y)
    return out


def lesser_kernel(green, sigma_in, first_list, second_list, green_t, sigma_t, own, first, second, flat, result):
    to_batch_lanes(green, flat, green_t)
    to_batch_lanes(sigma_in, flat, sigma_t)

    def store(p, g, half, value):
        result[p, half, :] = value

    sandwich(green_t, sigma_t, store)

    def regroup(q, carry):
        parts = swap_chunks([result[GROUPS * q + j] for j in range(GROUPS)])
        columns = pl.ds(pl.multiple_of(q * LANES, LANES), LANES)
        for h in range(GROUPS):
            own[h * NEAR : (h + 1) * NEAR, columns] = parts[h].astype(BF16)
        return carry

    lax.fori_loop(0, QUADS, regroup, 0, unroll=4)
    for listed, target in ((first_list, first), (second_list, second)):
        pick = (row_iota((64, 16)) == listed[...]).astype(BF16)
        for t in range(WIDTH // 512):
            columns = slice(t * 512, (t + 1) * 512)
            target[:, columns] = lax.dot_general(
                pick, own[:, columns], (((0,), (0,)), ((), ())), preferred_element_type=F32
            ).astype(BF16)


def mix_kernel(neighbours, coupling, own, low, high, mixed):
    names = lane_iota((64, 96))
    weights = jnp.zeros((64, 96), F32)
    for k in range(NBRS):
        weights = weights + jnp.where(names == neighbours[:, k : k + 1], coupling[:, k : k + 1], 0.0)
    coarse = weights.astype(BF16)
    fine = (weights - coarse.astype(F32)).astype(BF16)
    both = jnp.concatenate([coarse, fine], axis=1)
    for t in range(WIDTH // 512):
        columns = slice(t * 512, (t + 1) * 512)
        listed = [own[:, columns], low[:, columns], high[:, columns]]
        extended = jnp.concatenate(listed + listed, axis=0)
        mixed[:, columns] = jnp.dot(both, extended, preferred_element_type=F32).astype(BF16)


def band(offsets, w_emit, w_absorb):
    shape = (ROWS, LANES)
    distance = lane_iota(shape) % ROWS - row_iota(shape)
    before = jnp.zeros(shape, F32)
    here = jnp.zeros(shape, F32)
    after = jnp.zeros(shape, F32)
    for w in range(16):
        off, emit, absorb = offsets[w], w_emit[w], w_absorb[w]
        before = before + jnp.where(distance + ROWS == off, emit, 0.0)
        here = here + jnp.where(distance == off, emit, 0.0) + jnp.where(-distance == off, absorb, 0.0)
        after = after + jnp.where(ROWS - distance == off, absorb, 0.0)
    group = lane_iota(shape) // ROWS
    parts = []
    for block in (before, here, after):
        parts += [jnp.where(group == h, block, 0.0) for h in range(GROUPS)]
    return jnp.concatenate(parts, axis=0).astype(BF16)


def final_kernel(offsets, w_emit, w_absorb, green_t, sigma_t, before, here, after, sigma_ph, g_less, flat, middle, matrix):
    matrix[...] = band(offsets, w_emit, w_absorb)

    def convolve(q, carry):
        columns = pl.ds(pl.multiple_of(q * LANES, LANES), LANES)
        lhs = jnp.concatenate([before[:, columns], here[:, columns], after[:, columns]], axis=1)
        total = jnp.dot(lhs, matrix[...], preferred_element_type=F32).astype(BF16).astype(F32)
        parts = swap_chunks([total[h * NEAR : (h + 1) * NEAR] for h in range(GROUPS)])
        for j in range(GROUPS):
            p = GROUPS * q + j
            middle[p] = sigma_t[p] + parts[j]
            for g in range(2):
                flat[pl.ds(8 * g * PAIRS + p, 8, stride=PAIRS), :] = parts[j][8 * g : 8 * g + 8]
        return carry

    lax.fori_loop(0, QUADS, convolve, 0, unroll=4)
    to_energy_rows(flat, sigma_ph)

    def store(p, g, half, value):
        flat[pl.ds(g * 8 * PAIRS + p, 8, stride=PAIRS), :] = value

    sandwich(green_t, middle, store)
    to_energy_rows(flat, g_less)


def vmem(count):
    return [pl.BlockSpec(memory_space=pltpu.VMEM)] * count


def smem(count):
    return [pl.BlockSpec(memory_space=pltpu.SMEM)] * count


PARAMS = pltpu.CompilerParams(vmem_limit_bytes=48 * 1024 * 1024)


def swap(block, axis, parity):
    pairs = []
    for i in range(parity, lax.axis_size(axis) - 1, 2):
        pairs += [(i, i + 1), (i + 1, i)]
    return lax.ppermute(block, axis, pairs)


def on_device(green, sigma_in, neighbours, coupling, send_down, send_up, offsets, w_emit, w_absorb):
    odd_slab = lax.axis_index("slab") % 2 == 1
    odd_energy = lax.axis_index("energy") % 2 == 1
    first_list = jnp.where(odd_slab, send_down, send_up)
    second_list = jnp.where(odd_slab, send_up, send_down)
    whole = jax.ShapeDtypeStruct((PAIRS, NEAR, LANES), F32)
    edge = jax.ShapeDtypeStruct((16, WIDTH), BF16)
    block = jax.ShapeDtypeStruct((64, WIDTH), BF16)
    green_t, sigma_t, own, first, second = pl.pallas_call(
        lesser_kernel,
        out_shape=(whole, whole, block, edge, edge),
        in_specs=vmem(4),
        out_specs=tuple(vmem(5)),
        scratch_shapes=[pltpu.VMEM((SPAN, LANES), F32), pltpu.VMEM((PAIRS, NEAR, LANES), F32)],
        compiler_params=PARAMS,
    )(green, sigma_in, first_list, second_list)
    first = swap(first, "slab", 0)
    second = swap(second, "slab", 1)
    low = jnp.where(odd_slab, first, second)
    high = jnp.where(odd_slab, second, first)
    mixed = pl.pallas_call(
        mix_kernel,
        out_shape=block,
        in_specs=vmem(5),
        out_specs=vmem(1)[0],
        compiler_params=PARAMS,
    )(neighbours, coupling, own, low, high)
    apart = swap(mixed, "energy", 1)
    beside = swap(mixed, "energy", 0)
    before = jnp.where(odd_energy, beside, apart)
    after = jnp.where(odd_energy, apart, beside)
    flat = jax.ShapeDtypeStruct(green.shape, BF16)
    return pl.pallas_call(
        final_kernel,
        out_shape=(flat, flat),
        in_specs=smem(3) + vmem(5),
        out_specs=tuple(vmem(2)),
        scratch_shapes=[
            pltpu.VMEM((SPAN, LANES), F32),
            pltpu.VMEM((PAIRS, NEAR, LANES), F32),
            pltpu.VMEM((3 * LANES, LANES), BF16),
        ],
        compiler_params=PARAMS,
    )(offsets, w_emit, w_absorb, green_t, sigma_t, before, mixed, after)


def solution(mesh):
    split = P("energy", "slab")
    by_slab = P("slab", None)
    return jax.shard_map(
        on_device,
        mesh=mesh,
        in_specs=(split, split, by_slab, by_slab, by_slab, by_slab, P(), P(), P()),
        out_specs=(split, split),
        check_vma=False,
    )
```

```python
import jax
import jax.numpy as jnp
from jax import lax
from jax.experimental import pallas as pl
from jax.experimental.pallas import tpu as pltpu
from jax.sharding import PartitionSpec as P

ORB = 12
PAIRS = 144
NBRS = 8
FREQS = 16
LANES = 128
GROUPS = 4
ROWS = 32
ATOMS = 64
EDGE = 16
NEAR = 16
SPAN = NEAR * PAIRS
TILES = SPAN // LANES
QUADS = PAIRS // GROUPS
WIDTH = PAIRS * ROWS
WIDE = 512
BATCH = 12
F32 = jnp.float32
BF16 = jnp.bfloat16


def lane_iota(shape):
    return lax.broadcasted_iota(jnp.int32, shape, len(shape) - 1)


def row_iota(shape):
    return lax.broadcasted_iota(jnp.int32, shape, len(shape) - 2)


def identity(size):
    return (lane_iota((size, size)) == row_iota((size, size))).astype(BF16)


def matmul(lhs, rhs):
    return jnp.dot(lhs, rhs, preferred_element_type=F32)


def matmul_first(lhs, rhs):
    return lax.dot_general(lhs, rhs, (((0,), (0,)), ((), ())), preferred_element_type=F32)


def flip(eye, tile):
    return lax.dot_general(eye, tile, (((1,), (1,)), ((), ())), preferred_element_type=F32)


def to_batch_lanes(source, flat, target):
    eye = identity(LANES)
    for t in range(TILES):
        columns = [source[:, h * SPAN + t * LANES : h * SPAN + (t + 1) * LANES] for h in range(GROUPS)]
        flat[t * LANES : (t + 1) * LANES, :] = flip(eye, jnp.concatenate(columns, axis=0))
    for p in range(PAIRS):
        for g in range(2):
            target[p, 8 * g : 8 * g + 8, :] = flat[pl.ds(8 * g * PAIRS + p, 8, stride=PAIRS), :]


def to_energy_rows(flat, target, half):
    eye = identity(LANES)
    for t in range(half * TILES // 2, (half + 1) * TILES // 2):
        turned = flip(eye, flat[t * LANES : (t + 1) * LANES, :].astype(BF16)).astype(BF16)
        for h in range(GROUPS):
            column = h * SPAN + t * LANES
            target[:, column : column + LANES] = turned[h * ROWS : (h + 1) * ROWS]


def send_half(source, target, semaphores, half):
    copies = []
    for h in range(GROUPS):
        columns = pl.ds(h * SPAN + half * SPAN // 2, SPAN // 2)
        copy = pltpu.make_async_copy(source.at[:, columns], target.at[:, columns], semaphores.at[half * GROUPS + h])
        copy.start()
        copies.append(copy)
    return copies


def sandwich_half(left, middle, g, store):
    depth = 3
    half = slice(8 * g, 8 * g + 8)

    def body(step, carry):
        first = step * depth
        product = [[None] * ORB for _ in range(depth)]
        for j in range(ORB):
            lhs = [left[(first + r) * ORB + j, half, :] for r in range(depth)]
            for k in range(ORB):
                rhs = middle[j * ORB + k, half, :]
                for r in range(depth):
                    term = lhs[r] * rhs
                    product[r][k] = term if j == 0 else product[r][k] + term
        for l in range(ORB):
            total = [None] * depth
            for k in range(ORB):
                rhs = left[l * ORB + k, half, :]
                for r in range(depth):
                    term = product[r][k] * rhs
                    total[r] = term if k == 0 else total[r] + term
            for r in range(depth):
                store((first + r) * ORB + l, half, total[r])
        return carry

    lax.fori_loop(0, ORB // depth, body, 0)


def chunk_swap():
    distance = lane_iota((LANES, LANES)) - row_iota((LANES, LANES))
    group = row_iota((LANES, LANES)) // ROWS
    rows = []
    for a in range(GROUPS):
        row = [((distance == ROWS * (a - b)) & (group == b)).astype(BF16) for b in range(GROUPS)]
        rows.append(jnp.concatenate(row, axis=1))
    return jnp.concatenate(rows, axis=0)


def band(offsets, w_emit, w_absorb, odd):
    shape = (ROWS, LANES)
    distance = lane_iota(shape) % ROWS - row_iota(shape)
    before = jnp.zeros(shape, F32)
    here = jnp.zeros(shape, F32)
    after = jnp.zeros(shape, F32)
    for w in range(FREQS):
        off, emit, absorb = offsets[w], w_emit[w], w_absorb[w]
        before = before + jnp.where(distance + ROWS == off, emit, 0.0)
        here = here + jnp.where(distance == off, emit, 0.0) + jnp.where(-distance == off, absorb, 0.0)
        after = after + jnp.where(ROWS - distance == off, absorb, 0.0)
    apart = jnp.where(odd, after, before)
    beside = jnp.where(odd, before, after)
    group = lane_iota(shape) // ROWS
    parts = []
    for block in (apart, here, beside):
        parts += [jnp.where(group == h, block, 0.0) for h in range(GROUPS)]
    return jnp.concatenate(parts, axis=0).astype(BF16)


def atom_order(first_hot, second_hot):
    edge = jnp.maximum(jnp.max(first_hot, axis=1, keepdims=True), jnp.max(second_hot, axis=1, keepdims=True))
    shape = (ATOMS, ATOMS)
    earlier = jnp.sum(jnp.where(row_iota(shape) < lane_iota(shape), edge, 0.0), axis=0, keepdims=True)
    itself = jnp.sum(jnp.where(row_iota(shape) == lane_iota(shape), edge, 0.0), axis=0, keepdims=True)
    count = jnp.sum(jnp.broadcast_to(edge, shape), axis=0, keepdims=True)
    number = lane_iota((1, ATOMS)).astype(F32)
    place = jnp.where(itself > 0.5, earlier, count + number - earlier)
    return (row_iota(shape).astype(F32) == place).astype(BF16)


def mixing(neighbours, coupling, order, odd):
    names = row_iota((ATOMS + 2 * EDGE, ATOMS))
    weights = jnp.zeros((ATOMS + 2 * EDGE, ATOMS), F32)
    for k in range(NBRS):
        weights = weights + jnp.where(names == neighbours[k : k + 1, :], coupling[k : k + 1, :], 0.0)
    low, high = weights[ATOMS : ATOMS + EDGE], weights[ATOMS + EDGE :]
    edges = [jnp.where(odd, low, high), jnp.where(odd, high, low)]
    weights = jnp.concatenate([weights[:ATOMS]] + edges, axis=0)
    coarse = weights.astype(BF16)
    fine = (weights - coarse.astype(F32)).astype(BF16)
    rows = []
    for part in (coarse, fine):
        rows += [matmul(order, part[:ATOMS]).astype(BF16), part[ATOMS:]]
    return flip(identity(ATOMS), jnp.concatenate(rows, axis=0)).astype(BF16)


def lesser_kernel(
    green, sigma_in, *rest
):
    small = rest[:7]
    green_t, sigma_t, own, near, far, matrix, weights, pick, swapper = rest[7:16]
    held = rest[16:23]
    green_here, sigma_here, flat, result, grouped, semaphores, small_semaphores = rest[23:]
    copies = []
    fetched = []
    for n, (source, target) in enumerate(zip(small, held)):
        copy = pltpu.make_async_copy(source, target, small_semaphores.at[n])
        copy.start()
        fetched.append(copy)
    for n, (source, target) in enumerate(((green, green_here), (sigma_in, sigma_here))):
        for h in range(GROUPS):
            columns = pl.ds(h * SPAN, SPAN)
            copy = pltpu.make_async_copy(
                source.at[:, columns], target.at[:, columns], semaphores.at[n * GROUPS + h]
            )
            copy.start()
            copies.append(copy)
    swapper[...] = chunk_swap()
    for copy in fetched:
        copy.wait()
    offsets, w_emit, w_absorb, neighbours, coupling, send_down, send_up = held
    odd_slab = lax.axis_index("slab") % 2 == 1
    odd_energy = lax.axis_index("energy") % 2 == 1
    down_hot = (row_iota((ATOMS, EDGE)) == send_down[...]).astype(F32)
    up_hot = (row_iota((ATOMS, EDGE)) == send_up[...]).astype(F32)
    first_hot = jnp.where(odd_slab, down_hot, up_hot)
    second_hot = jnp.where(odd_slab, up_hot, down_hot)
    order = atom_order(first_hot, second_hot)
    hot = jnp.concatenate([first_hot, second_hot], axis=1).astype(BF16)
    pick[...] = matmul(order[: 2 * EDGE], hot).astype(BF16)
    weights[...] = mixing(neighbours, coupling, order, odd_slab)
    matrix[...] = band(offsets, w_emit, w_absorb, odd_energy)
    for copy in copies[:GROUPS]:
        copy.wait()
    to_batch_lanes(green_here, flat, green_t)
    for copy in copies[GROUPS:]:
        copy.wait()
    to_batch_lanes(sigma_here, flat, sigma_t)

    def store(p, half, value):
        result[p, half, :] = value

    for g in range(2):
        sandwich_half(green_t, sigma_t, g, store)
    for base in range(0, QUADS, BATCH):
        columns = []
        for j in range(GROUPS):
            columns.append(jnp.concatenate(
                [result[GROUPS * q + j].astype(BF16) for q in range(base, base + BATCH)], axis=0
            ))
        moved = matmul(jnp.concatenate(columns, axis=1), swapper[...]).astype(BF16)
        for i in range(BATCH):
            for h in range(GROUPS):
                grouped[h * NEAR : (h + 1) * NEAR, (base + i) * LANES : (base + i + 1) * LANES] = moved[
                    i * NEAR : (i + 1) * NEAR, h * LANES : (h + 1) * LANES
                ]
    for t in range(WIDTH // WIDE):
        columns = slice(t * WIDE, (t + 1) * WIDE)
        ordered = matmul(order, grouped[:, columns]).astype(BF16)
        own[:, columns] = ordered
        near[:, columns] = ordered[: 2 * EDGE]
        far[:, columns] = ordered[2 * EDGE :]


def convolve(matrix, apart, here, beside, target):
    for base in range(0, QUADS, BATCH):
        lhs = []
        for source in (apart, here, beside):
            lhs.append(jnp.concatenate(
                [source[:, q * LANES : (q + 1) * LANES] for q in range(base, base + BATCH)], axis=0
            ))
        total = matmul(jnp.concatenate(lhs, axis=1), matrix[...]).astype(BF16)
        for i in range(BATCH):
            column = (base + i) * LANES
            target[:, column : column + LANES] = total[i * 2 * EDGE : (i + 1) * 2 * EDGE]


def near_kernel(matrix, pick, apart, here, beside, target, first, second):
    convolve(matrix, apart, here, beside.at[: 2 * EDGE, :], target)
    for t in range(WIDTH // WIDE):
        columns = slice(t * WIDE, (t + 1) * WIDE)
        picked = matmul_first(pick[...], target[:, columns]).astype(BF16)
        first[:, columns] = picked[:EDGE]
        second[:, columns] = picked[EDGE:]


def far_kernel(matrix, apart, here, beside, target):
    convolve(matrix, apart, here, beside.at[2 * EDGE :, :], target)


def final_kernel(
    weights, swapper, near, far, first, second, green_t, sigma_t, sigma_ph, g_less,
    flat, flat_less, middle, sigma_here, less_here, semaphores, less_semaphores,
):
    for base in range(0, QUADS, BATCH):
        parts = []
        for t in range(base * LANES // WIDE, (base + BATCH) * LANES // WIDE):
            columns = slice(t * WIDE, (t + 1) * WIDE)
            listed = [near[:, columns], far[:, columns], first[:, columns], second[:, columns]]
            extended = jnp.concatenate(listed + listed, axis=0)
            parts.append(matmul(weights[...], extended).astype(BF16))
        mixed = jnp.concatenate(parts, axis=1)
        columns = []
        for h in range(GROUPS):
            columns.append(jnp.concatenate(
                [mixed[h * NEAR : (h + 1) * NEAR, i * LANES : (i + 1) * LANES] for i in range(BATCH)], axis=0
            ))
        moved = matmul(jnp.concatenate(columns, axis=1), swapper[...])
        for i in range(BATCH):
            for j in range(GROUPS):
                p = GROUPS * (base + i) + j
                part = moved[i * NEAR : (i + 1) * NEAR, j * LANES : (j + 1) * LANES]
                middle[p] = sigma_t[p] + part
                for g in range(2):
                    flat[pl.ds(8 * g * PAIRS + p, 8, stride=PAIRS), :] = part[8 * g : 8 * g + 8]
    copies = []
    for g in range(2):
        to_energy_rows(flat, sigma_here, g)
        copies += send_half(sigma_here, sigma_ph, semaphores, g)

    for g in range(2):
        def store(p, half, value):
            flat_less[pl.ds(8 * g * PAIRS + p, 8, stride=PAIRS), :] = value

        sandwich_half(green_t, middle, g, store)
        to_energy_rows(flat_less, less_here, g)
        copies += send_half(less_here, g_less, less_semaphores, g)
    for copy in copies:
        copy.wait()


def vmem(count):
    return [pl.BlockSpec(memory_space=pltpu.VMEM)] * count


def anywhere(count):
    return [pl.BlockSpec(memory_space=pl.ANY)] * count


PARAMS = pltpu.CompilerParams(vmem_limit_bytes=44 * 1024 * 1024)


def swap(block, axis, parity):
    pairs = []
    for i in range(parity, lax.axis_size(axis) - 1, 2):
        pairs += [(i, i + 1), (i + 1, i)]
    return lax.ppermute(block, axis, pairs)


def shape_of(*shape, kind=BF16):
    return jax.ShapeDtypeStruct(shape, kind)


def on_device(green, sigma_in, neighbours, coupling, send_down, send_up, offsets, w_emit, w_absorb):
    whole = shape_of(PAIRS, NEAR, LANES, kind=F32)
    half = shape_of(2 * EDGE, WIDTH)
    edge = shape_of(EDGE, WIDTH)
    given = (green, sigma_in, offsets, w_emit, w_absorb, neighbours.T, coupling.T, send_down, send_up)
    given = [pltpu.with_memory_space_constraint(array, pltpu.HBM) for array in given]
    green_t, sigma_t, own, near, far, matrix, weights, pick, swapper = pl.pallas_call(
        lesser_kernel,
        out_shape=(
            whole, whole, shape_of(ATOMS, WIDTH), half, half, shape_of(3 * LANES, LANES),
            shape_of(ATOMS, 2 * (ATOMS + 2 * EDGE)), shape_of(2 * EDGE, 2 * EDGE), shape_of(WIDE, WIDE),
        ),
        in_specs=anywhere(9),
        out_specs=tuple(vmem(9)),
        scratch_shapes=[
            pltpu.SMEM((FREQS,), jnp.int32),
            pltpu.SMEM((FREQS,), F32),
            pltpu.SMEM((FREQS,), F32),
            pltpu.VMEM((NBRS, ATOMS), jnp.int32),
            pltpu.VMEM((NBRS, ATOMS), F32),
            pltpu.VMEM((1, EDGE), jnp.int32),
            pltpu.VMEM((1, EDGE), jnp.int32),
            pltpu.VMEM((ROWS, ATOMS * PAIRS), BF16),
            pltpu.VMEM((ROWS, ATOMS * PAIRS), BF16),
            pltpu.VMEM((SPAN, LANES), F32),
            pltpu.VMEM((PAIRS, NEAR, LANES), F32),
            pltpu.VMEM((ATOMS, WIDTH), BF16),
            pltpu.SemaphoreType.DMA((2 * GROUPS,)),
            pltpu.SemaphoreType.DMA((7,)),
        ],
        compiler_params=PARAMS,
    )(*given)
    near_apart = swap(near, "energy", 1)
    far_apart = swap(far, "energy", 1)
    beside = swap(own, "energy", 0)
    near_done, first, second = pl.pallas_call(
        near_kernel,
        out_shape=(half, edge, edge),
        in_specs=vmem(5),
        out_specs=tuple(vmem(3)),
        compiler_params=PARAMS,
    )(matrix, pick, near_apart, near, beside)
    first = swap(first, "slab", 0)
    second = swap(second, "slab", 1)
    far_done = pl.pallas_call(
        far_kernel,
        out_shape=half,
        in_specs=vmem(4),
        out_specs=vmem(1)[0],
        compiler_params=PARAMS,
    )(matrix, far_apart, far, beside)
    flat = shape_of(ROWS, ATOMS * PAIRS)
    return pl.pallas_call(
        final_kernel,
        out_shape=(flat, flat),
        in_specs=vmem(8),
        out_specs=tuple(anywhere(2)),
        scratch_shapes=[
            pltpu.VMEM((SPAN, LANES), F32),
            pltpu.VMEM((SPAN, LANES), F32),
            pltpu.VMEM((PAIRS, NEAR, LANES), F32),
            pltpu.VMEM((ROWS, ATOMS * PAIRS), BF16),
            pltpu.VMEM((ROWS, ATOMS * PAIRS), BF16),
            pltpu.SemaphoreType.DMA((2 * GROUPS,)),
            pltpu.SemaphoreType.DMA((2 * GROUPS,)),
        ],
        compiler_params=PARAMS,
    )(weights, swapper, near_done, far_done, first, second, green_t, sigma_t)


def solution(mesh):
    split = P("energy", "slab")
    by_slab = P("slab", None)
    return jax.shard_map(
        on_device,
        mesh=mesh,
        in_specs=(split, split, by_slab, by_slab, by_slab, by_slab, P(), P(), P()),
        out_specs=(split, split),
        check_vma=False,
    )
```

```python
import jax
import jax.numpy as jnp
from jax import lax
from jax.experimental import pallas as pl
from jax.experimental.pallas import tpu as pltpu
from jax.sharding import PartitionSpec as P

ORB = 12
PAIRS = 144
NBRS = 8
FREQS = 16
LANES = 128
GROUPS = 4
ROWS = 32
ATOMS = 64
EDGE = 16
NEAR = 16
SPAN = NEAR * PAIRS
PITCH = PAIRS + 1
TILES = SPAN // LANES
QUADS = PAIRS // GROUPS
WIDTH = PAIRS * ROWS
WIDE = 512
BATCH = 12
F32 = jnp.float32
BF16 = jnp.bfloat16


def lane_iota(shape):
    return lax.broadcasted_iota(jnp.int32, shape, len(shape) - 1)


def row_iota(shape):
    return lax.broadcasted_iota(jnp.int32, shape, len(shape) - 2)


def identity(size):
    return (lane_iota((size, size)) == row_iota((size, size))).astype(BF16)


def matmul(lhs, rhs):
    return jnp.dot(lhs, rhs, preferred_element_type=F32)


def matmul_first(lhs, rhs):
    return lax.dot_general(lhs, rhs, (((0,), (0,)), ((), ())), preferred_element_type=F32)


def flip(eye, tile):
    return lax.dot_general(eye, tile, (((1,), (1,)), ((), ())), preferred_element_type=F32)


def pieces(t):
    row, stop = t * LANES, (t + 1) * LANES
    while row < stop:
        atom = row // PAIRS
        size = min(stop, (atom + 1) * PAIRS) - row
        yield row - t * LANES, row + atom * (PITCH - PAIRS), size
        row += size


def atom_rows(p, g):
    return pl.ds(8 * g * PITCH + p, 8, stride=PITCH)


def to_batch_lanes(source, target, half):
    for t in range(half * TILES // 2, (half + 1) * TILES // 2):
        columns = [source[:, h * SPAN + t * LANES : h * SPAN + (t + 1) * LANES] for h in range(GROUPS)]
        turned = jnp.concatenate(columns, axis=0).T.astype(F32)
        for start, row, size in pieces(t):
            target[row : row + size, :] = turned[start : start + size]


def to_energy_rows(flat, target, half):
    for t in range(half * TILES // 2, (half + 1) * TILES // 2):
        rows = [flat[row : row + size, :].astype(BF16) for _, row, size in pieces(t)]
        turned = jnp.concatenate(rows, axis=0).T
        for h in range(GROUPS):
            column = h * SPAN + t * LANES
            target[:, column : column + LANES] = turned[h * ROWS : (h + 1) * ROWS]


def move_half(source, target, semaphores, half):
    copies = []
    for h in range(GROUPS):
        columns = pl.ds(h * SPAN + half * SPAN // 2, SPAN // 2)
        copy = pltpu.make_async_copy(source.at[:, columns], target.at[:, columns], semaphores.at[half * GROUPS + h])
        copy.start()
        copies.append(copy)
    return copies


def sandwich_half(left, middle, g, store):
    depth = 3
    def body(step, carry):
        first = step * depth
        product = [[None] * ORB for _ in range(depth)]
        for j in range(ORB):
            lhs = [left[atom_rows((first + r) * ORB + j, g), :] for r in range(depth)]
            for k in range(ORB):
                rhs = middle[atom_rows(j * ORB + k, g), :]
                for r in range(depth):
                    term = lhs[r] * rhs
                    product[r][k] = term if j == 0 else product[r][k] + term
        for l in range(ORB):
            total = [None] * depth
            for k in range(ORB):
                rhs = left[atom_rows(l * ORB + k, g), :]
                for r in range(depth):
                    term = product[r][k] * rhs
                    total[r] = term if k == 0 else total[r] + term
            for r in range(depth):
                store((first + r) * ORB + l, total[r])
        return carry

    lax.fori_loop(0, ORB // depth, body, 0)


def chunk_swap():
    distance = lane_iota((LANES, LANES)) - row_iota((LANES, LANES))
    group = row_iota((LANES, LANES)) // ROWS
    rows = []
    for a in range(GROUPS):
        row = [((distance == ROWS * (a - b)) & (group == b)).astype(BF16) for b in range(GROUPS)]
        rows.append(jnp.concatenate(row, axis=1))
    return jnp.concatenate(rows, axis=0)


def band(offsets, w_emit, w_absorb, odd):
    shape = (ROWS, LANES)
    distance = lane_iota(shape) % ROWS - row_iota(shape)
    before = jnp.zeros(shape, F32)
    here = jnp.zeros(shape, F32)
    after = jnp.zeros(shape, F32)
    for w in range(FREQS):
        off, emit, absorb = offsets[w], w_emit[w], w_absorb[w]
        before = before + jnp.where(distance + ROWS == off, emit, 0.0)
        here = here + jnp.where(distance == off, emit, 0.0) + jnp.where(-distance == off, absorb, 0.0)
        after = after + jnp.where(ROWS - distance == off, absorb, 0.0)
    apart = jnp.where(odd, after, before)
    beside = jnp.where(odd, before, after)
    group = lane_iota(shape) // ROWS
    parts = []
    for block in (apart, here, beside):
        parts += [jnp.where(group == h, block, 0.0) for h in range(GROUPS)]
    return jnp.concatenate(parts, axis=0).astype(BF16)


def atom_order(first_hot, second_hot):
    edge = jnp.maximum(jnp.max(first_hot, axis=1, keepdims=True), jnp.max(second_hot, axis=1, keepdims=True))
    shape = (ATOMS, ATOMS)
    earlier = jnp.sum(jnp.where(row_iota(shape) < lane_iota(shape), edge, 0.0), axis=0, keepdims=True)
    itself = jnp.sum(jnp.where(row_iota(shape) == lane_iota(shape), edge, 0.0), axis=0, keepdims=True)
    count = jnp.sum(jnp.broadcast_to(edge, shape), axis=0, keepdims=True)
    number = lane_iota((1, ATOMS)).astype(F32)
    place = jnp.where(itself > 0.5, earlier, count + number - earlier)
    return (row_iota(shape).astype(F32) == place).astype(BF16)


def mixing(neighbours, coupling, order, odd):
    names = row_iota((ATOMS + 2 * EDGE, ATOMS))
    weights = jnp.zeros((ATOMS + 2 * EDGE, ATOMS), F32)
    for k in range(NBRS):
        weights = weights + jnp.where(names == neighbours[k : k + 1, :], coupling[k : k + 1, :], 0.0)
    low, high = weights[ATOMS : ATOMS + EDGE], weights[ATOMS + EDGE :]
    edges = [jnp.where(odd, low, high), jnp.where(odd, high, low)]
    weights = jnp.concatenate([weights[:ATOMS]] + edges, axis=0)
    coarse = weights.astype(BF16)
    fine = (weights - coarse.astype(F32)).astype(BF16)
    own = [matmul(order, part[:ATOMS]).astype(BF16) for part in (coarse, fine)]
    edge = [part[ATOMS:] for part in (coarse, fine)]
    return [flip(identity(ATOMS), jnp.concatenate(rows, axis=0)).astype(BF16) for rows in (own, edge)]


def lesser_kernel(
    green, sigma_in, *rest
):
    small = rest[:7]
    green_t, sigma_t, near, far, matrix, own_weights, edge_weights, pick, swapper = rest[7:16]
    held = rest[16:23]
    green_here, sigma_here, result, grouped, green_semaphores, sigma_semaphores, small_semaphores = rest[23:]
    copies = []
    fetched = []
    for n, (source, target) in enumerate(zip(small, held)):
        copy = pltpu.make_async_copy(source, target, small_semaphores.at[n])
        copy.start()
        fetched.append(copy)
    for source, target, semaphores in ((green, green_here, green_semaphores), (sigma_in, sigma_here, sigma_semaphores)):
        copies += [move_half(source, target, semaphores, g) for g in range(2)]
    swapper[...] = chunk_swap()
    for copy in fetched:
        copy.wait()
    offsets, w_emit, w_absorb, neighbours, coupling, send_down, send_up = held
    odd_slab = lax.axis_index("slab") % 2 == 1
    odd_energy = lax.axis_index("energy") % 2 == 1
    down_hot = (row_iota((ATOMS, EDGE)) == send_down[...]).astype(F32)
    up_hot = (row_iota((ATOMS, EDGE)) == send_up[...]).astype(F32)
    first_hot = jnp.where(odd_slab, down_hot, up_hot)
    second_hot = jnp.where(odd_slab, up_hot, down_hot)
    order = atom_order(first_hot, second_hot)
    hot = jnp.concatenate([first_hot, second_hot], axis=1).astype(BF16)
    pick[...] = matmul(order[: 2 * EDGE], hot).astype(BF16)
    own_weights[...], edge_weights[...] = mixing(neighbours, coupling, order, odd_slab)
    matrix[...] = band(offsets, w_emit, w_absorb, odd_energy)
    for n, (source, target) in enumerate(((green_here, green_t), (sigma_here, sigma_t))):
        for g in range(2):
            for copy in copies[2 * n + g]:
                copy.wait()
            to_batch_lanes(source, target, g)
    for g in range(2):
        def store(p, value):
            result[p, 8 * g : 8 * g + 8, :] = value

        sandwich_half(green_t, sigma_t, g, store)
    for base in range(0, QUADS, BATCH):
        columns = []
        for j in range(GROUPS):
            columns.append(jnp.concatenate(
                [result[GROUPS * q + j].astype(BF16) for q in range(base, base + BATCH)], axis=0
            ))
        moved = matmul(jnp.concatenate(columns, axis=1), swapper[...]).astype(BF16)
        for i in range(BATCH):
            for h in range(GROUPS):
                grouped[h * NEAR : (h + 1) * NEAR, (base + i) * LANES : (base + i + 1) * LANES] = moved[
                    i * NEAR : (i + 1) * NEAR, h * LANES : (h + 1) * LANES
                ]
    for t in range(WIDTH // WIDE):
        columns = slice(t * WIDE, (t + 1) * WIDE)
        ordered = matmul(order, grouped[:, columns]).astype(BF16)
        near[:, columns] = ordered[: 2 * EDGE]
        far[:, columns] = ordered[2 * EDGE :]


def convolve(matrix, apart, here, beside, target):
    for base in range(0, QUADS, BATCH):
        lhs = []
        for source in (apart, here, beside):
            lhs.append(jnp.concatenate(
                [source[:, q * LANES : (q + 1) * LANES] for q in range(base, base + BATCH)], axis=0
            ))
        total = matmul(jnp.concatenate(lhs, axis=1), matrix[...]).astype(BF16)
        for i in range(BATCH):
            column = (base + i) * LANES
            target[:, column : column + LANES] = total[i * 2 * EDGE : (i + 1) * 2 * EDGE]


def near_kernel(matrix, pick, apart, here, beside, target, first, second):
    convolve(matrix, apart, here, beside, target)
    for t in range(WIDTH // WIDE):
        columns = slice(t * WIDE, (t + 1) * WIDE)
        picked = matmul_first(pick[...], target[:, columns]).astype(BF16)
        first[:, columns] = picked[:EDGE]
        second[:, columns] = picked[EDGE:]


def far_kernel(matrix, weights, near, apart, here, beside, mixed, target):
    convolve(matrix, apart, here, beside, target)
    for t in range(WIDTH // WIDE):
        columns = slice(t * WIDE, (t + 1) * WIDE)
        listed = [near[:, columns], target[:, columns]]
        mixed[:, columns] = matmul(weights[...], jnp.concatenate(listed + listed, axis=0))


def final_kernel(
    weights, swapper, own, first, second, green_t, sigma_t, sigma_ph, g_less,
    flat, flat_less, middle, sigma_here, less_here, semaphores, less_semaphores,
):
    for base in range(0, QUADS, BATCH):
        parts = []
        for t in range(base * LANES // WIDE, (base + BATCH) * LANES // WIDE):
            columns = slice(t * WIDE, (t + 1) * WIDE)
            listed = [first[:, columns], second[:, columns]]
            edges = matmul(weights[...], jnp.concatenate(listed + listed, axis=0))
            parts.append((own[:, columns] + edges).astype(BF16))
        mixed = jnp.concatenate(parts, axis=1)
        columns = []
        for h in range(GROUPS):
            columns.append(jnp.concatenate(
                [mixed[h * NEAR : (h + 1) * NEAR, i * LANES : (i + 1) * LANES] for i in range(BATCH)], axis=0
            ))
        moved = matmul(jnp.concatenate(columns, axis=1), swapper[...])
        for i in range(BATCH):
            for j in range(GROUPS):
                part = moved[i * NEAR : (i + 1) * NEAR, j * LANES : (j + 1) * LANES]
                for g in range(2):
                    rows = atom_rows(GROUPS * (base + i) + j, g)
                    flat[rows, :] = part[8 * g : 8 * g + 8]
                    middle[rows, :] = sigma_t[rows, :] + part[8 * g : 8 * g + 8]
    copies = []
    for g in range(2):
        to_energy_rows(flat, sigma_here, g)
        copies += move_half(sigma_here, sigma_ph, semaphores, g)

    for g in range(2):
        def store(p, value):
            flat_less[atom_rows(p, g), :] = value

        sandwich_half(green_t, middle, g, store)
        to_energy_rows(flat_less, less_here, g)
        copies += move_half(less_here, g_less, less_semaphores, g)
    for copy in copies:
        copy.wait()


def vmem(count):
    return [pl.BlockSpec(memory_space=pltpu.VMEM)] * count


def anywhere(count):
    return [pl.BlockSpec(memory_space=pl.ANY)] * count


PARAMS = pltpu.CompilerParams(vmem_limit_bytes=44 * 1024 * 1024)


def swap(block, axis, parity):
    pairs = []
    for i in range(parity, lax.axis_size(axis) - 1, 2):
        pairs += [(i, i + 1), (i + 1, i)]
    return lax.ppermute(block, axis, pairs)


def shape_of(*shape, kind=BF16):
    return jax.ShapeDtypeStruct(shape, kind)


def on_device(green, sigma_in, neighbours, coupling, send_down, send_up, offsets, w_emit, w_absorb):
    tall = shape_of(NEAR * PITCH, LANES, kind=F32)
    half = shape_of(2 * EDGE, WIDTH)
    edge = shape_of(EDGE, WIDTH)
    given = (green, sigma_in, offsets, w_emit, w_absorb, neighbours.T, coupling.T, send_down, send_up)
    given = [pltpu.with_memory_space_constraint(array, pltpu.HBM) for array in given]
    green_t, sigma_t, near, far, matrix, own_weights, edge_weights, pick, swapper = pl.pallas_call(
        lesser_kernel,
        out_shape=(
            tall, tall, half, half, shape_of(3 * LANES, LANES), shape_of(ATOMS, 2 * ATOMS),
            shape_of(ATOMS, 4 * EDGE), shape_of(2 * EDGE, 2 * EDGE), shape_of(WIDE, WIDE),
        ),
        in_specs=anywhere(9),
        out_specs=tuple(vmem(9)),
        scratch_shapes=[
            pltpu.SMEM((FREQS,), jnp.int32),
            pltpu.SMEM((FREQS,), F32),
            pltpu.SMEM((FREQS,), F32),
            pltpu.VMEM((NBRS, ATOMS), jnp.int32),
            pltpu.VMEM((NBRS, ATOMS), F32),
            pltpu.VMEM((1, EDGE), jnp.int32),
            pltpu.VMEM((1, EDGE), jnp.int32),
            pltpu.VMEM((ROWS, ATOMS * PAIRS), BF16),
            pltpu.VMEM((ROWS, ATOMS * PAIRS), BF16),
            pltpu.VMEM((PAIRS, NEAR, LANES), F32),
            pltpu.VMEM((ATOMS, WIDTH), BF16),
            pltpu.SemaphoreType.DMA((2 * GROUPS,)),
            pltpu.SemaphoreType.DMA((2 * GROUPS,)),
            pltpu.SemaphoreType.DMA((7,)),
        ],
        compiler_params=PARAMS,
    )(*given)
    near_apart = swap(near, "energy", 1)
    near_beside = swap(near, "energy", 0)
    far_apart = swap(far, "energy", 1)
    far_beside = swap(far, "energy", 0)
    near_done, first, second = pl.pallas_call(
        near_kernel,
        out_shape=(half, edge, edge),
        in_specs=vmem(5),
        out_specs=tuple(vmem(3)),
        compiler_params=PARAMS,
    )(matrix, pick, near_apart, near, near_beside)
    first = swap(first, "slab", 0)
    second = swap(second, "slab", 1)
    own = pl.pallas_call(
        far_kernel,
        out_shape=shape_of(ATOMS, WIDTH, kind=F32),
        in_specs=vmem(6),
        out_specs=vmem(1)[0],
        scratch_shapes=[pltpu.VMEM((2 * EDGE, WIDTH), BF16)],
        compiler_params=PARAMS,
    )(matrix, own_weights, near_done, far_apart, far, far_beside)
    flat = shape_of(ROWS, ATOMS * PAIRS)
    return pl.pallas_call(
        final_kernel,
        out_shape=(flat, flat),
        in_specs=vmem(7),
        out_specs=tuple(anywhere(2)),
        scratch_shapes=[
            pltpu.VMEM((NEAR * PITCH, LANES), F32),
            pltpu.VMEM((NEAR * PITCH, LANES), F32),
            pltpu.VMEM((NEAR * PITCH, LANES), F32),
            pltpu.VMEM((ROWS, ATOMS * PAIRS), BF16),
            pltpu.VMEM((ROWS, ATOMS * PAIRS), BF16),
            pltpu.SemaphoreType.DMA((2 * GROUPS,)),
            pltpu.SemaphoreType.DMA((2 * GROUPS,)),
        ],
        compiler_params=PARAMS,
    )(edge_weights, swapper, own, first, second, green_t, sigma_t)


def solution(mesh):
    split = P("energy", "slab")
    by_slab = P("slab", None)
    return jax.shard_map(
        on_device,
        mesh=mesh,
        in_specs=(split, split, by_slab, by_slab, by_slab, by_slab, P(), P(), P()),
        out_specs=(split, split),
        check_vma=False,
    )
```

```python
import jax
import jax.numpy as jnp
from jax import lax
from jax.experimental import pallas as pl
from jax.experimental.pallas import tpu as pltpu
from jax.sharding import PartitionSpec as P

ORB = 12
PAIRS = 144
NBRS = 8
FREQS = 16
LANES = 128
GROUPS = 4
ROWS = 32
ATOMS = 64
EDGE = 16
NEAR = 16
SPAN = NEAR * PAIRS
PITCH = PAIRS + 1
TILES = SPAN // LANES
QUADS = PAIRS // GROUPS
WIDTH = PAIRS * ROWS
WIDE = 512
BATCH = 12
F32 = jnp.float32
BF16 = jnp.bfloat16


def lane_iota(shape):
    return lax.broadcasted_iota(jnp.int32, shape, len(shape) - 1)


def row_iota(shape):
    return lax.broadcasted_iota(jnp.int32, shape, len(shape) - 2)


def identity(size):
    return (lane_iota((size, size)) == row_iota((size, size))).astype(BF16)


def matmul(lhs, rhs):
    return jnp.dot(lhs, rhs, preferred_element_type=F32)


def matmul_first(lhs, rhs):
    return lax.dot_general(lhs, rhs, (((0,), (0,)), ((), ())), preferred_element_type=F32)


def flip(eye, tile):
    return lax.dot_general(eye, tile, (((1,), (1,)), ((), ())), preferred_element_type=F32)


def pieces(t):
    row, stop = t * LANES, (t + 1) * LANES
    while row < stop:
        atom = row // PAIRS
        size = min(stop, (atom + 1) * PAIRS) - row
        yield row - t * LANES, row + atom * (PITCH - PAIRS), size
        row += size


def atom_rows(p, g):
    return pl.ds(8 * g * PITCH + p, 8, stride=PITCH)


def to_batch_lanes(source, target, half):
    for t in range(half * TILES // 2, (half + 1) * TILES // 2):
        columns = [source[:, h * SPAN + t * LANES : h * SPAN + (t + 1) * LANES] for h in range(GROUPS)]
        turned = jnp.concatenate(columns, axis=0).T.astype(F32)
        for start, row, size in pieces(t):
            target[row : row + size, :] = turned[start : start + size]


def to_energy_rows(flat, target, half):
    for t in range(half * TILES // 2, (half + 1) * TILES // 2):
        rows = [flat[row : row + size, :].astype(BF16) for _, row, size in pieces(t)]
        turned = jnp.concatenate(rows, axis=0).T
        for h in range(GROUPS):
            column = h * SPAN + t * LANES
            target[:, column : column + LANES] = turned[h * ROWS : (h + 1) * ROWS]


def move_half(source, target, semaphores, half):
    copies = []
    for h in range(GROUPS):
        columns = pl.ds(h * SPAN + half * SPAN // 2, SPAN // 2)
        copy = pltpu.make_async_copy(source.at[:, columns], target.at[:, columns], semaphores.at[half * GROUPS + h])
        copy.start()
        copies.append(copy)
    return copies


def sandwich_half(left, middle, g, store):
    depth = 3
    def body(step, carry):
        first = step * depth
        product = [[None] * ORB for _ in range(depth)]
        for j in range(ORB):
            lhs = [left[atom_rows((first + r) * ORB + j, g), :] for r in range(depth)]
            for k in range(ORB):
                rhs = middle[atom_rows(j * ORB + k, g), :]
                for r in range(depth):
                    term = lhs[r] * rhs
                    product[r][k] = term if j == 0 else product[r][k] + term
        for l in range(ORB):
            total = [None] * depth
            for k in range(ORB):
                rhs = left[atom_rows(l * ORB + k, g), :]
                for r in range(depth):
                    term = product[r][k] * rhs
                    total[r] = term if k == 0 else total[r] + term
            for r in range(depth):
                store((first + r) * ORB + l, total[r])
        return carry

    lax.fori_loop(0, ORB // depth, body, 0)


def chunk_swap():
    distance = lane_iota((LANES, LANES)) - row_iota((LANES, LANES))
    group = row_iota((LANES, LANES)) // ROWS
    rows = []
    for a in range(GROUPS):
        row = [((distance == ROWS * (a - b)) & (group == b)).astype(BF16) for b in range(GROUPS)]
        rows.append(jnp.concatenate(row, axis=1))
    return jnp.concatenate(rows, axis=0)


def band(offsets, w_emit, w_absorb, odd, end):
    shape = (ROWS, LANES)
    distance = lane_iota(shape) % ROWS - row_iota(shape)
    before = jnp.zeros(shape, F32)
    here = jnp.zeros(shape, F32)
    after = jnp.zeros(shape, F32)
    for w in range(FREQS):
        off, emit, absorb = offsets[w], w_emit[w], w_absorb[w]
        before = before + jnp.where(distance + ROWS == off, emit, 0.0)
        here = here + jnp.where(distance == off, emit, 0.0) + jnp.where(-distance == off, absorb, 0.0)
        after = after + jnp.where(ROWS - distance == off, absorb, 0.0)
    apart = jnp.where(end, 0.0, jnp.where(odd, after, before))
    beside = jnp.where(odd, before, after)
    group = lane_iota(shape) // ROWS
    parts = []
    for block in (apart, here, beside):
        parts += [jnp.where(group == h, block, 0.0) for h in range(GROUPS)]
    return jnp.concatenate(parts, axis=0).astype(BF16)


def atom_order(first_hot, second_hot):
    edge = jnp.maximum(jnp.max(first_hot, axis=1, keepdims=True), jnp.max(second_hot, axis=1, keepdims=True))
    shape = (ATOMS, ATOMS)
    earlier = jnp.sum(jnp.where(row_iota(shape) < lane_iota(shape), edge, 0.0), axis=0, keepdims=True)
    itself = jnp.sum(jnp.where(row_iota(shape) == lane_iota(shape), edge, 0.0), axis=0, keepdims=True)
    count = jnp.sum(jnp.broadcast_to(edge, shape), axis=0, keepdims=True)
    number = lane_iota((1, ATOMS)).astype(F32)
    place = jnp.where(itself > 0.5, earlier, count + number - earlier)
    return (row_iota(shape).astype(F32) == place).astype(BF16)


def mixing(neighbours, coupling, order, odd, lowest, highest):
    names = row_iota((ATOMS + 2 * EDGE, ATOMS))
    weights = jnp.zeros((ATOMS + 2 * EDGE, ATOMS), F32)
    for k in range(NBRS):
        weights = weights + jnp.where(names == neighbours[k : k + 1, :], coupling[k : k + 1, :], 0.0)
    low = jnp.where(lowest, 0.0, weights[ATOMS : ATOMS + EDGE])
    high = jnp.where(highest, 0.0, weights[ATOMS + EDGE :])
    edges = [jnp.where(odd, low, high), jnp.where(odd, high, low)]
    weights = jnp.concatenate([weights[:ATOMS]] + edges, axis=0)
    coarse = weights.astype(BF16)
    fine = (weights - coarse.astype(F32)).astype(BF16)
    own = [matmul(order, part[:ATOMS]).astype(BF16) for part in (coarse, fine)]
    edge = [part[ATOMS:] for part in (coarse, fine)]
    return [flip(identity(ATOMS), jnp.concatenate(rows, axis=0)).astype(BF16) for rows in (own, edge)]


def lesser_kernel(
    green, sigma_in, *rest
):
    small = rest[:7]
    green_t, sigma_t, near, far, matrix, own_weights, edge_weights, pick, swapper = rest[7:16]
    held = rest[16:23]
    green_here, sigma_here, result, grouped, green_semaphores, sigma_semaphores, small_semaphores = rest[23:]
    copies = []
    fetched = []
    for n, (source, target) in enumerate(zip(small, held)):
        copy = pltpu.make_async_copy(source, target, small_semaphores.at[n])
        copy.start()
        fetched.append(copy)
    for source, target, semaphores in ((green, green_here, green_semaphores), (sigma_in, sigma_here, sigma_semaphores)):
        copies += [move_half(source, target, semaphores, g) for g in range(2)]
    swapper[...] = chunk_swap()
    for copy in fetched:
        copy.wait()
    offsets, w_emit, w_absorb, neighbours, coupling, send_down, send_up = held
    slab, energy = lax.axis_index("slab"), lax.axis_index("energy")
    odd_energy = energy % 2 == 1
    below = slab % 2 == 1
    lowest, highest = slab == 0, slab == lax.axis_size("slab") - 1
    end_energy = (energy == 0) | (energy == lax.axis_size("energy") - 1)
    down_hot = (row_iota((ATOMS, EDGE)) == send_down[...]).astype(F32)
    up_hot = (row_iota((ATOMS, EDGE)) == send_up[...]).astype(F32)
    first_hot = jnp.where(below, down_hot, up_hot)
    second_hot = jnp.where(below, up_hot, down_hot)
    order = atom_order(first_hot, second_hot)
    hot = jnp.concatenate([first_hot, second_hot], axis=1).astype(BF16)
    pick[...] = matmul(order[: 2 * EDGE], hot).astype(BF16)
    own_weights[...], edge_weights[...] = mixing(neighbours, coupling, order, below, lowest, highest)
    matrix[...] = band(offsets, w_emit, w_absorb, odd_energy, end_energy)
    for n, (source, target) in enumerate(((green_here, green_t), (sigma_here, sigma_t))):
        for g in range(2):
            for copy in copies[2 * n + g]:
                copy.wait()
            to_batch_lanes(source, target, g)
    for g in range(2):
        def store(p, value):
            result[p, 8 * g : 8 * g + 8, :] = value

        sandwich_half(green_t, sigma_t, g, store)
    for base in range(0, QUADS, BATCH):
        columns = []
        for j in range(GROUPS):
            columns.append(jnp.concatenate(
                [result[GROUPS * q + j].astype(BF16) for q in range(base, base + BATCH)], axis=0
            ))
        moved = matmul(jnp.concatenate(columns, axis=1), swapper[...]).astype(BF16)
        for i in range(BATCH):
            for h in range(GROUPS):
                grouped[h * NEAR : (h + 1) * NEAR, (base + i) * LANES : (base + i + 1) * LANES] = moved[
                    i * NEAR : (i + 1) * NEAR, h * LANES : (h + 1) * LANES
                ]
    for t in range(WIDTH // WIDE):
        columns = slice(t * WIDE, (t + 1) * WIDE)
        ordered = matmul(order, grouped[:, columns]).astype(BF16)
        near[:, columns] = ordered[: 2 * EDGE]
        far[:, columns] = ordered[2 * EDGE :]


def convolve(matrix, apart, here, beside, target):
    for base in range(0, QUADS, BATCH):
        lhs = []
        for source in (apart, here, beside):
            lhs.append(jnp.concatenate(
                [source[:, q * LANES : (q + 1) * LANES] for q in range(base, base + BATCH)], axis=0
            ))
        total = matmul(jnp.concatenate(lhs, axis=1), matrix[...]).astype(BF16)
        for i in range(BATCH):
            column = (base + i) * LANES
            target[:, column : column + LANES] = total[i * 2 * EDGE : (i + 1) * 2 * EDGE]


def near_kernel(matrix, pick, apart, here, beside, target, first, second):
    convolve(matrix, apart, here, beside, target)
    for t in range(WIDTH // WIDE):
        columns = slice(t * WIDE, (t + 1) * WIDE)
        picked = matmul_first(pick[...], target[:, columns]).astype(BF16)
        first[:, columns] = picked[:EDGE]
        second[:, columns] = picked[EDGE:]


def far_kernel(matrix, weights, near, apart, here, beside, mixed, target):
    convolve(matrix, apart, here, beside, target)
    for t in range(WIDTH // WIDE):
        columns = slice(t * WIDE, (t + 1) * WIDE)
        listed = [near[:, columns], target[:, columns]]
        mixed[:, columns] = matmul(weights[...], jnp.concatenate(listed + listed, axis=0))


def final_kernel(
    weights, swapper, own, first, second, green_t, sigma_t, sigma_ph, g_less,
    flat, flat_less, middle, sigma_here, less_here, semaphores, less_semaphores,
):
    for base in range(0, QUADS, BATCH):
        parts = []
        for t in range(base * LANES // WIDE, (base + BATCH) * LANES // WIDE):
            columns = slice(t * WIDE, (t + 1) * WIDE)
            listed = [first[:, columns], second[:, columns]]
            edges = matmul(weights[...], jnp.concatenate(listed + listed, axis=0))
            parts.append((own[:, columns] + edges).astype(BF16))
        mixed = jnp.concatenate(parts, axis=1)
        columns = []
        for h in range(GROUPS):
            columns.append(jnp.concatenate(
                [mixed[h * NEAR : (h + 1) * NEAR, i * LANES : (i + 1) * LANES] for i in range(BATCH)], axis=0
            ))
        moved = matmul(jnp.concatenate(columns, axis=1), swapper[...])
        for i in range(BATCH):
            for j in range(GROUPS):
                part = moved[i * NEAR : (i + 1) * NEAR, j * LANES : (j + 1) * LANES]
                for g in range(2):
                    rows = atom_rows(GROUPS * (base + i) + j, g)
                    flat[rows, :] = part[8 * g : 8 * g + 8]
                    middle[rows, :] = sigma_t[rows, :] + part[8 * g : 8 * g + 8]
    copies = []
    for g in range(2):
        to_energy_rows(flat, sigma_here, g)
        copies += move_half(sigma_here, sigma_ph, semaphores, g)

    for g in range(2):
        def store(p, value):
            flat_less[atom_rows(p, g), :] = value

        sandwich_half(green_t, middle, g, store)
        to_energy_rows(flat_less, less_here, g)
        copies += move_half(less_here, g_less, less_semaphores, g)
    for copy in copies:
        copy.wait()


def vmem(count):
    return [pl.BlockSpec(memory_space=pltpu.VMEM)] * count


def anywhere(count):
    return [pl.BlockSpec(memory_space=pl.ANY)] * count


PARAMS = pltpu.CompilerParams(vmem_limit_bytes=44 * 1024 * 1024)


def pair_up(block, partner):
    energies, slabs = lax.axis_size("energy"), lax.axis_size("slab")
    pairs = []
    for energy in range(energies):
        for slab in range(slabs):
            other_energy, other_slab = partner(energy, slab, energies, slabs)
            pairs.append((energy * slabs + slab, other_energy * slabs + other_slab))
    return lax.ppermute(block, ("energy", "slab"), pairs)


def beside(energy, slab, energies, slabs):
    return energy ^ 1, slab


def apart(energy, slab, energies, slabs):
    other = ((energy + 1) ^ 1) - 1
    if 0 <= other < energies:
        return other, slab
    return energy, slab ^ 1


def slab_step(energy, slab, slabs, step, aside):
    if 0 <= slab + step < slabs:
        return energy, slab + step
    return energy ^ aside, slab


def first_slab(energy, slab, energies, slabs):
    return slab_step(energy, slab, slabs, 1 if slab % 2 == 0 else -1, 1)


def second_slab(energy, slab, energies, slabs):
    return slab_step(energy, slab, slabs, -1 if slab % 2 == 0 else 1, 1)


def shape_of(*shape, kind=BF16):
    return jax.ShapeDtypeStruct(shape, kind)


def on_device(green, sigma_in, neighbours, coupling, send_down, send_up, offsets, w_emit, w_absorb):
    tall = shape_of(NEAR * PITCH, LANES, kind=F32)
    half = shape_of(2 * EDGE, WIDTH)
    edge = shape_of(EDGE, WIDTH)
    given = (green, sigma_in, offsets, w_emit, w_absorb, neighbours.T, coupling.T, send_down, send_up)
    given = [pltpu.with_memory_space_constraint(array, pltpu.HBM) for array in given]
    green_t, sigma_t, near, far, matrix, own_weights, edge_weights, pick, swapper = pl.pallas_call(
        lesser_kernel,
        out_shape=(
            tall, tall, half, half, shape_of(3 * LANES, LANES), shape_of(ATOMS, 2 * ATOMS),
            shape_of(ATOMS, 4 * EDGE), shape_of(2 * EDGE, 2 * EDGE), shape_of(WIDE, WIDE),
        ),
        in_specs=anywhere(9),
        out_specs=tuple(vmem(9)),
        scratch_shapes=[
            pltpu.SMEM((FREQS,), jnp.int32),
            pltpu.SMEM((FREQS,), F32),
            pltpu.SMEM((FREQS,), F32),
            pltpu.VMEM((NBRS, ATOMS), jnp.int32),
            pltpu.VMEM((NBRS, ATOMS), F32),
            pltpu.VMEM((1, EDGE), jnp.int32),
            pltpu.VMEM((1, EDGE), jnp.int32),
            pltpu.VMEM((ROWS, ATOMS * PAIRS), BF16),
            pltpu.VMEM((ROWS, ATOMS * PAIRS), BF16),
            pltpu.VMEM((PAIRS, NEAR, LANES), F32),
            pltpu.VMEM((ATOMS, WIDTH), BF16),
            pltpu.SemaphoreType.DMA((2 * GROUPS,)),
            pltpu.SemaphoreType.DMA((2 * GROUPS,)),
            pltpu.SemaphoreType.DMA((7,)),
        ],
        compiler_params=PARAMS,
    )(*given)
    near_apart = pair_up(near, apart)
    near_beside = pair_up(near, beside)
    far_apart = pair_up(far, apart)
    far_beside = pair_up(far, beside)
    near_done, first, second = pl.pallas_call(
        near_kernel,
        out_shape=(half, edge, edge),
        in_specs=vmem(5),
        out_specs=tuple(vmem(3)),
        compiler_params=PARAMS,
    )(matrix, pick, near_apart, near, near_beside)
    first = pair_up(first, first_slab)
    second = pair_up(second, second_slab)
    own = pl.pallas_call(
        far_kernel,
        out_shape=shape_of(ATOMS, WIDTH, kind=F32),
        in_specs=vmem(6),
        out_specs=vmem(1)[0],
        scratch_shapes=[pltpu.VMEM((2 * EDGE, WIDTH), BF16)],
        compiler_params=PARAMS,
    )(matrix, own_weights, near_done, far_apart, far, far_beside)
    flat = shape_of(ROWS, ATOMS * PAIRS)
    return pl.pallas_call(
        final_kernel,
        out_shape=(flat, flat),
        in_specs=vmem(7),
        out_specs=tuple(anywhere(2)),
        scratch_shapes=[
            pltpu.VMEM((NEAR * PITCH, LANES), F32),
            pltpu.VMEM((NEAR * PITCH, LANES), F32),
            pltpu.VMEM((NEAR * PITCH, LANES), F32),
            pltpu.VMEM((ROWS, ATOMS * PAIRS), BF16),
            pltpu.VMEM((ROWS, ATOMS * PAIRS), BF16),
            pltpu.SemaphoreType.DMA((2 * GROUPS,)),
            pltpu.SemaphoreType.DMA((2 * GROUPS,)),
        ],
        compiler_params=PARAMS,
    )(edge_weights, swapper, own, first, second, green_t, sigma_t)


def solution(mesh):
    split = P("energy", "slab")
    by_slab = P("slab", None)
    return jax.shard_map(
        on_device,
        mesh=mesh,
        in_specs=(split, split, by_slab, by_slab, by_slab, by_slab, P(), P(), P()),
        out_specs=(split, split),
        check_vma=False,
    )
```

```python
import jax
import jax.numpy as jnp
from jax import lax
from jax.experimental import pallas as pl
from jax.experimental.pallas import tpu as pltpu
from jax.sharding import PartitionSpec as P

ORB = 12
PAIRS = 144
NBRS = 8
FREQS = 16
LANES = 128
GROUPS = 4
ROWS = 32
ATOMS = 64
EDGE = 16
REST = ATOMS - EDGE
NAMED = ATOMS + EDGE
NEAR = 16
SPAN = NEAR * PAIRS
PITCH = PAIRS + 1
TILES = SPAN // LANES
QUADS = PAIRS // GROUPS
WIDTH = PAIRS * ROWS
WIDE = 512
BATCH = 12
F32 = jnp.float32
BF16 = jnp.bfloat16


def lane_iota(shape):
    return lax.broadcasted_iota(jnp.int32, shape, len(shape) - 1)


def row_iota(shape):
    return lax.broadcasted_iota(jnp.int32, shape, len(shape) - 2)


def identity(size):
    return (lane_iota((size, size)) == row_iota((size, size))).astype(BF16)


def matmul(lhs, rhs):
    return jnp.dot(lhs, rhs, preferred_element_type=F32)


def matmul_first(lhs, rhs):
    return lax.dot_general(lhs, rhs, (((0,), (0,)), ((), ())), preferred_element_type=F32)


def flip(eye, tile):
    return lax.dot_general(eye, tile, (((1,), (1,)), ((), ())), preferred_element_type=F32)


def pieces(t):
    row, stop = t * LANES, (t + 1) * LANES
    while row < stop:
        atom = row // PAIRS
        size = min(stop, (atom + 1) * PAIRS) - row
        yield row - t * LANES, row + atom * (PITCH - PAIRS), size
        row += size


def atom_rows(p, g):
    return pl.ds(8 * g * PITCH + p, 8, stride=PITCH)


def to_batch_lanes(source, target, half):
    for t in range(half * TILES // 2, (half + 1) * TILES // 2):
        columns = [source[:, h * SPAN + t * LANES : h * SPAN + (t + 1) * LANES] for h in range(GROUPS)]
        turned = jnp.concatenate(columns, axis=0).T.astype(F32)
        for start, row, size in pieces(t):
            target[row : row + size, :] = turned[start : start + size]


def to_energy_rows(flat, target, half):
    for t in range(half * TILES // 2, (half + 1) * TILES // 2):
        rows = [flat[row : row + size, :].astype(BF16) for _, row, size in pieces(t)]
        turned = jnp.concatenate(rows, axis=0).T
        for h in range(GROUPS):
            column = h * SPAN + t * LANES
            target[:, column : column + LANES] = turned[h * ROWS : (h + 1) * ROWS]


def move_half(source, target, semaphores, half):
    copies = []
    for h in range(GROUPS):
        columns = pl.ds(h * SPAN + half * SPAN // 2, SPAN // 2)
        copy = pltpu.make_async_copy(source.at[:, columns], target.at[:, columns], semaphores.at[half * GROUPS + h])
        copy.start()
        copies.append(copy)
    return copies


def sandwich_half(left, middle, g, store):
    depth = 3
    def body(step, carry):
        first = step * depth
        product = [[None] * ORB for _ in range(depth)]
        for j in range(ORB):
            lhs = [left[atom_rows((first + r) * ORB + j, g), :] for r in range(depth)]
            for k in range(ORB):
                rhs = middle[atom_rows(j * ORB + k, g), :]
                for r in range(depth):
                    term = lhs[r] * rhs
                    product[r][k] = term if j == 0 else product[r][k] + term
        for l in range(ORB):
            total = [None] * depth
            for k in range(ORB):
                rhs = left[atom_rows(l * ORB + k, g), :]
                for r in range(depth):
                    term = product[r][k] * rhs
                    total[r] = term if k == 0 else total[r] + term
            for r in range(depth):
                store((first + r) * ORB + l, total[r])
        return carry

    lax.fori_loop(0, ORB // depth, body, 0)


def chunk_swap():
    distance = lane_iota((LANES, LANES)) - row_iota((LANES, LANES))
    group = row_iota((LANES, LANES)) // ROWS
    rows = []
    for a in range(GROUPS):
        row = [((distance == ROWS * (a - b)) & (group == b)).astype(BF16) for b in range(GROUPS)]
        rows.append(jnp.concatenate(row, axis=1))
    return jnp.concatenate(rows, axis=0)


def band(offsets, w_emit, w_absorb, odd, end):
    shape = (ROWS, LANES)
    distance = lane_iota(shape) % ROWS - row_iota(shape)
    before = jnp.zeros(shape, F32)
    here = jnp.zeros(shape, F32)
    after = jnp.zeros(shape, F32)
    for w in range(FREQS):
        off, emit, absorb = offsets[w], w_emit[w], w_absorb[w]
        before = before + jnp.where(distance + ROWS == off, emit, 0.0)
        here = here + jnp.where(distance == off, emit, 0.0) + jnp.where(-distance == off, absorb, 0.0)
        after = after + jnp.where(ROWS - distance == off, absorb, 0.0)
    apart = jnp.where(end, 0.0, jnp.where(odd, after, before))
    beside = jnp.where(odd, before, after)
    group = lane_iota(shape) // ROWS
    parts = []
    for block in (apart, here, beside):
        parts += [jnp.where(group == h, block, 0.0) for h in range(GROUPS)]
    return jnp.concatenate(parts, axis=0).astype(BF16)


def atom_order(first_hot, second_hot):
    in_first = jnp.max(first_hot, axis=1, keepdims=True)
    edge = jnp.maximum(in_first, jnp.max(second_hot, axis=1, keepdims=True))
    shape = (ATOMS, ATOMS)
    earlier = jnp.sum(jnp.where(row_iota(shape) < lane_iota(shape), edge, 0.0), axis=0, keepdims=True)
    itself = row_iota(shape) == lane_iota(shape)
    in_edge = jnp.sum(jnp.where(itself, edge, 0.0), axis=0, keepdims=True)
    in_first = jnp.sum(jnp.where(itself, in_first, 0.0), axis=0, keepdims=True)
    place = jnp.where(in_edge > 0.5, -1.0, lane_iota((1, ATOMS)).astype(F32) - earlier)
    rest = (row_iota((REST, ATOMS)).astype(F32) == place).astype(BF16)
    eye = identity(EDGE)
    first = flip(eye, first_hot.astype(BF16))
    second = flip(eye, second_hot.astype(BF16))
    order = jnp.concatenate([first.astype(BF16), second.astype(BF16), rest], axis=0)
    once = jnp.concatenate([first.astype(BF16), (second * (1.0 - in_first)).astype(BF16), rest], axis=0)
    return order, once


def mixing(neighbours, coupling, order, odd, lowest, highest):
    names = row_iota((ATOMS + 2 * EDGE, ATOMS))
    weights = jnp.zeros((ATOMS + 2 * EDGE, ATOMS), F32)
    for k in range(NBRS):
        weights = weights + jnp.where(names == neighbours[k : k + 1, :], coupling[k : k + 1, :], 0.0)
    low = jnp.where(lowest, 0.0, weights[ATOMS : ATOMS + EDGE])
    high = jnp.where(highest, 0.0, weights[ATOMS + EDGE :])
    edges = [jnp.where(odd, low, high), jnp.where(odd, high, low)]
    weights = jnp.concatenate([weights[:ATOMS]] + edges, axis=0)
    coarse = weights.astype(BF16)
    fine = (weights - coarse.astype(F32)).astype(BF16)
    own = [matmul(order, part[:ATOMS]).astype(BF16) for part in (coarse, fine)]
    edge = [part[ATOMS:] for part in (coarse, fine)]
    return [flip(identity(ATOMS), jnp.concatenate(rows, axis=0)).astype(BF16) for rows in (own, edge)]


def lesser_kernel(
    green, sigma_in, down_list, up_list, green_t, sigma_t, near, far, once, swapper,
    send_down, send_up, green_here, sigma_here, result, grouped, green_semaphores, sigma_semaphores, small_semaphores,
):
    copies = []
    fetched = []
    for n, (source, target) in enumerate(((down_list, send_down), (up_list, send_up))):
        copy = pltpu.make_async_copy(source, target, small_semaphores.at[n])
        copy.start()
        fetched.append(copy)
    for source, target, semaphores in ((green, green_here, green_semaphores), (sigma_in, sigma_here, sigma_semaphores)):
        copies += [move_half(source, target, semaphores, g) for g in range(2)]
    swapper[...] = chunk_swap()
    for copy in fetched:
        copy.wait()
    below = lax.axis_index("slab") % 2 == 1
    down_hot = (row_iota((ATOMS, EDGE)) == send_down[...]).astype(F32)
    up_hot = (row_iota((ATOMS, EDGE)) == send_up[...]).astype(F32)
    order, once[...] = atom_order(jnp.where(below, down_hot, up_hot), jnp.where(below, up_hot, down_hot))
    for n, (source, target) in enumerate(((green_here, green_t), (sigma_here, sigma_t))):
        for g in range(2):
            for copy in copies[2 * n + g]:
                copy.wait()
            to_batch_lanes(source, target, g)
    for g in range(2):
        def store(p, value):
            result[p, 8 * g : 8 * g + 8, :] = value

        sandwich_half(green_t, sigma_t, g, store)
    for base in range(0, QUADS, BATCH):
        columns = []
        for j in range(GROUPS):
            columns.append(jnp.concatenate(
                [result[GROUPS * q + j].astype(BF16) for q in range(base, base + BATCH)], axis=0
            ))
        moved = matmul(jnp.concatenate(columns, axis=1), swapper[...]).astype(BF16)
        for i in range(BATCH):
            for h in range(GROUPS):
                grouped[h * NEAR : (h + 1) * NEAR, (base + i) * LANES : (base + i + 1) * LANES] = moved[
                    i * NEAR : (i + 1) * NEAR, h * LANES : (h + 1) * LANES
                ]
    for t in range(WIDTH // WIDE):
        columns = slice(t * WIDE, (t + 1) * WIDE)
        ordered = matmul(order, grouped[:, columns]).astype(BF16)
        near[:, columns] = ordered[: 2 * EDGE]
        far[:, columns] = ordered[2 * EDGE :]


def stack(source, base):
    return jnp.concatenate([source[:, q * LANES : (q + 1) * LANES] for q in range(base, base + BATCH)], axis=0)


def here_kernel(
    offset_list, emit_list, absorb_list, neighbour_list, coupling_list, once, near, near_beside,
    matrix, own_weights, edge_weights, partial, offsets, w_emit, w_absorb, neighbours, coupling, semaphores,
):
    sources = (offset_list, emit_list, absorb_list, neighbour_list, coupling_list)
    targets = (offsets, w_emit, w_absorb, neighbours, coupling)
    copies = []
    for n, (source, target) in enumerate(zip(sources, targets)):
        copy = pltpu.make_async_copy(source, target, semaphores.at[n])
        copy.start()
        copies.append(copy)
    for copy in copies:
        copy.wait()
    slab, energy = lax.axis_index("slab"), lax.axis_index("energy")
    lowest, highest = slab == 0, slab == lax.axis_size("slab") - 1
    end_energy = (energy == 0) | (energy == lax.axis_size("energy") - 1)
    own_weights[...], edge_weights[...] = mixing(neighbours, coupling, once[...], slab % 2 == 1, lowest, highest)
    matrix[...] = band(offsets, w_emit, w_absorb, energy % 2 == 1, end_energy)
    for base in range(0, QUADS, BATCH):
        lhs = jnp.concatenate([stack(near, base), stack(near_beside, base)], axis=1)
        total = matmul(lhs, matrix[LANES:, :])
        for i in range(BATCH):
            column = (base + i) * LANES
            partial[:, column : column + LANES] = total[i * 2 * EDGE : (i + 1) * 2 * EDGE]


def near_kernel(matrix, near_apart, partial, first, second):
    for base in range(0, QUADS, BATCH):
        total = matmul(stack(near_apart, base), matrix[:LANES, :])
        for i in range(BATCH):
            columns = slice((base + i) * LANES, (base + i + 1) * LANES)
            whole = (partial[:, columns] + total[i * 2 * EDGE : (i + 1) * 2 * EDGE]).astype(BF16)
            first[:, columns] = whole[:EDGE]
            second[:, columns] = whole[EDGE:]


def far_kernel(matrix, weights, first, second, far_apart, far, far_beside, mixed, target):
    for base in range(0, QUADS, BATCH):
        lhs = jnp.concatenate([stack(source, base) for source in (far_apart, far, far_beside)], axis=1)
        total = matmul(lhs, matrix[...]).astype(BF16)
        for i in range(BATCH):
            column = (base + i) * LANES
            target[:, column : column + LANES] = total[i * REST : (i + 1) * REST]
    for t in range(WIDTH // WIDE):
        columns = slice(t * WIDE, (t + 1) * WIDE)
        listed = [first[:, columns], second[:, columns], target[:, columns]]
        mixed[:, columns] = matmul(weights[...], jnp.concatenate(listed + listed, axis=0))


def final_kernel(
    weights, swapper, own, first, second, green_t, sigma_t, sigma_ph, g_less,
    flat, flat_less, middle, sigma_here, less_here, semaphores, less_semaphores,
):
    for base in range(0, QUADS, BATCH):
        parts = []
        for t in range(base * LANES // WIDE, (base + BATCH) * LANES // WIDE):
            columns = slice(t * WIDE, (t + 1) * WIDE)
            listed = [first[:, columns], second[:, columns]]
            edges = matmul(weights[...], jnp.concatenate(listed + listed, axis=0))
            parts.append((own[:, columns] + edges).astype(BF16))
        mixed = jnp.concatenate(parts, axis=1)
        columns = []
        for h in range(GROUPS):
            columns.append(jnp.concatenate(
                [mixed[h * NEAR : (h + 1) * NEAR, i * LANES : (i + 1) * LANES] for i in range(BATCH)], axis=0
            ))
        moved = matmul(jnp.concatenate(columns, axis=1), swapper[...])
        for i in range(BATCH):
            for j in range(GROUPS):
                part = moved[i * NEAR : (i + 1) * NEAR, j * LANES : (j + 1) * LANES]
                for g in range(2):
                    rows = atom_rows(GROUPS * (base + i) + j, g)
                    flat[rows, :] = part[8 * g : 8 * g + 8]
                    middle[rows, :] = sigma_t[rows, :] + part[8 * g : 8 * g + 8]
    copies = []
    for g in range(2):
        to_energy_rows(flat, sigma_here, g)
        copies += move_half(sigma_here, sigma_ph, semaphores, g)

    for g in range(2):
        def store(p, value):
            flat_less[atom_rows(p, g), :] = value

        sandwich_half(green_t, middle, g, store)
        to_energy_rows(flat_less, less_here, g)
        copies += move_half(less_here, g_less, less_semaphores, g)
    for copy in copies:
        copy.wait()


def vmem(count):
    return [pl.BlockSpec(memory_space=pltpu.VMEM)] * count


def anywhere(count):
    return [pl.BlockSpec(memory_space=pl.ANY)] * count


PARAMS = pltpu.CompilerParams(vmem_limit_bytes=44 * 1024 * 1024)


def pair_up(block, partner):
    energies, slabs = lax.axis_size("energy"), lax.axis_size("slab")
    pairs = []
    for energy in range(energies):
        for slab in range(slabs):
            other_energy, other_slab = partner(energy, slab, energies, slabs)
            pairs.append((energy * slabs + slab, other_energy * slabs + other_slab))
    return lax.ppermute(block, ("energy", "slab"), pairs)


def beside(energy, slab, energies, slabs):
    return energy ^ 1, slab


def apart(energy, slab, energies, slabs):
    other = ((energy + 1) ^ 1) - 1
    if 0 <= other < energies:
        return other, slab
    return energy, slab ^ 1


def slab_step(energy, slab, slabs, step, aside):
    if 0 <= slab + step < slabs:
        return energy, slab + step
    return energy ^ aside, slab


def first_slab(energy, slab, energies, slabs):
    return slab_step(energy, slab, slabs, 1 if slab % 2 == 0 else -1, 1)


def second_slab(energy, slab, energies, slabs):
    return slab_step(energy, slab, slabs, -1 if slab % 2 == 0 else 1, 1)


def shape_of(*shape, kind=BF16):
    return jax.ShapeDtypeStruct(shape, kind)


def in_hbm(arrays):
    return [pltpu.with_memory_space_constraint(array, pltpu.HBM) for array in arrays]


def on_device(green, sigma_in, neighbours, coupling, send_down, send_up, offsets, w_emit, w_absorb):
    tall = shape_of(NEAR * PITCH, LANES, kind=F32)
    half = shape_of(2 * EDGE, WIDTH)
    edge = shape_of(EDGE, WIDTH)
    green_t, sigma_t, near, far, once, swapper = pl.pallas_call(
        lesser_kernel,
        out_shape=(tall, tall, half, shape_of(REST, WIDTH), shape_of(NAMED, ATOMS), shape_of(WIDE, WIDE)),
        in_specs=anywhere(4),
        out_specs=tuple(vmem(6)),
        scratch_shapes=[
            pltpu.VMEM((1, EDGE), jnp.int32),
            pltpu.VMEM((1, EDGE), jnp.int32),
            pltpu.VMEM((ROWS, ATOMS * PAIRS), BF16),
            pltpu.VMEM((ROWS, ATOMS * PAIRS), BF16),
            pltpu.VMEM((PAIRS, NEAR, LANES), F32),
            pltpu.VMEM((ATOMS, WIDTH), BF16),
            pltpu.SemaphoreType.DMA((2 * GROUPS,)),
            pltpu.SemaphoreType.DMA((2 * GROUPS,)),
            pltpu.SemaphoreType.DMA((2,)),
        ],
        compiler_params=PARAMS,
    )(*in_hbm((green, sigma_in, send_down, send_up)))
    near_apart = pair_up(near, apart)
    near_beside = pair_up(near, beside)
    far_apart = pair_up(far, apart)
    far_beside = pair_up(far, beside)
    matrix, own_weights, edge_weights, partial = pl.pallas_call(
        here_kernel,
        out_shape=(
            shape_of(3 * LANES, LANES), shape_of(ATOMS, 2 * NAMED), shape_of(ATOMS, 4 * EDGE),
            shape_of(2 * EDGE, WIDTH, kind=F32),
        ),
        in_specs=anywhere(5) + vmem(3),
        out_specs=tuple(vmem(4)),
        scratch_shapes=[
            pltpu.SMEM((FREQS,), jnp.int32),
            pltpu.SMEM((FREQS,), F32),
            pltpu.SMEM((FREQS,), F32),
            pltpu.VMEM((NBRS, ATOMS), jnp.int32),
            pltpu.VMEM((NBRS, ATOMS), F32),
            pltpu.SemaphoreType.DMA((5,)),
        ],
        compiler_params=PARAMS,
    )(*in_hbm((offsets, w_emit, w_absorb, neighbours.T, coupling.T)), once, near, near_beside)
    first, second = pl.pallas_call(
        near_kernel,
        out_shape=(edge, edge),
        in_specs=vmem(3),
        out_specs=tuple(vmem(2)),
        compiler_params=PARAMS,
    )(matrix, near_apart, partial)
    own = pl.pallas_call(
        far_kernel,
        out_shape=shape_of(ATOMS, WIDTH, kind=F32),
        in_specs=vmem(7),
        out_specs=vmem(1)[0],
        scratch_shapes=[pltpu.VMEM((REST, WIDTH), BF16)],
        compiler_params=PARAMS,
    )(matrix, own_weights, first, second, far_apart, far, far_beside)
    first = pair_up(first, first_slab)
    second = pair_up(second, second_slab)
    flat = shape_of(ROWS, ATOMS * PAIRS)
    return pl.pallas_call(
        final_kernel,
        out_shape=(flat, flat),
        in_specs=vmem(7),
        out_specs=tuple(anywhere(2)),
        scratch_shapes=[
            pltpu.VMEM((NEAR * PITCH, LANES), F32),
            pltpu.VMEM((NEAR * PITCH, LANES), F32),
            pltpu.VMEM((NEAR * PITCH, LANES), F32),
            pltpu.VMEM((ROWS, ATOMS * PAIRS), BF16),
            pltpu.VMEM((ROWS, ATOMS * PAIRS), BF16),
            pltpu.SemaphoreType.DMA((2 * GROUPS,)),
            pltpu.SemaphoreType.DMA((2 * GROUPS,)),
        ],
        compiler_params=PARAMS,
    )(edge_weights, swapper, own, first, second, green_t, sigma_t)


def solution(mesh):
    split = P("energy", "slab")
    by_slab = P("slab", None)
    return jax.shard_map(
        on_device,
        mesh=mesh,
        in_specs=(split, split, by_slab, by_slab, by_slab, by_slab, P(), P(), P()),
        out_specs=(split, split),
        check_vma=False,
    )
```

```python
import jax
import jax.numpy as jnp
from jax import lax
from jax.experimental import pallas as pl
from jax.experimental.pallas import tpu as pltpu
from jax.sharding import PartitionSpec as P

ORB = 12
PAIRS = 144
NBRS = 8
FREQS = 16
LANES = 128
GROUPS = 4
ROWS = 32
ATOMS = 64
EDGE = 16
REST = ATOMS - EDGE
NAMED = ATOMS + EDGE
NEAR = 16
SPAN = NEAR * PAIRS
PITCH = PAIRS + 1
TILES = SPAN // LANES
QUADS = PAIRS // GROUPS
WIDTH = PAIRS * ROWS
WIDE = 512
BATCH = 12
LAST = 36
F32 = jnp.float32
BF16 = jnp.bfloat16


def lane_iota(shape):
    return lax.broadcasted_iota(jnp.int32, shape, len(shape) - 1)


def row_iota(shape):
    return lax.broadcasted_iota(jnp.int32, shape, len(shape) - 2)


def identity(size):
    return (lane_iota((size, size)) == row_iota((size, size))).astype(BF16)


def matmul(lhs, rhs):
    return jnp.dot(lhs, rhs, preferred_element_type=F32)


def matmul_first(lhs, rhs):
    return lax.dot_general(lhs, rhs, (((0,), (0,)), ((), ())), preferred_element_type=F32)


def flip(eye, tile):
    return lax.dot_general(eye, tile, (((1,), (1,)), ((), ())), preferred_element_type=F32)


def pieces(t):
    row, stop = t * LANES, (t + 1) * LANES
    while row < stop:
        atom = row // PAIRS
        size = min(stop, (atom + 1) * PAIRS) - row
        yield row - t * LANES, row + atom * (PITCH - PAIRS), size
        row += size


def atom_rows(p, g):
    return pl.ds(8 * g * PITCH + p, 8, stride=PITCH)


def to_batch_lanes(source, target, half):
    for t in range(half * TILES // 2, (half + 1) * TILES // 2):
        columns = [source[:, h * SPAN + t * LANES : h * SPAN + (t + 1) * LANES] for h in range(GROUPS)]
        turned = jnp.concatenate(columns, axis=0).T.astype(F32)
        for start, row, size in pieces(t):
            target[row : row + size, :] = turned[start : start + size]


def to_energy_rows(flat, target, half):
    for t in range(half * TILES // 2, (half + 1) * TILES // 2):
        rows = [flat[row : row + size, :].astype(BF16) for _, row, size in pieces(t)]
        turned = jnp.concatenate(rows, axis=0).T
        for h in range(GROUPS):
            column = h * SPAN + t * LANES
            target[:, column : column + LANES] = turned[h * ROWS : (h + 1) * ROWS]


def move_half(source, target, semaphores, half):
    copies = []
    for h in range(GROUPS):
        columns = pl.ds(h * SPAN + half * SPAN // 2, SPAN // 2)
        copy = pltpu.make_async_copy(source.at[:, columns], target.at[:, columns], semaphores.at[half * GROUPS + h])
        copy.start()
        copies.append(copy)
    return copies


def sandwich_half(left, middle, g, store):
    depth = 3
    def body(step, carry):
        first = step * depth
        product = [[None] * ORB for _ in range(depth)]
        for j in range(ORB):
            lhs = [left[atom_rows((first + r) * ORB + j, g), :] for r in range(depth)]
            for k in range(ORB):
                rhs = middle[atom_rows(j * ORB + k, g), :]
                for r in range(depth):
                    term = lhs[r] * rhs
                    product[r][k] = term if j == 0 else product[r][k] + term
        for l in range(ORB):
            total = [None] * depth
            for k in range(ORB):
                rhs = left[atom_rows(l * ORB + k, g), :]
                for r in range(depth):
                    term = product[r][k] * rhs
                    total[r] = term if k == 0 else total[r] + term
            for r in range(depth):
                store((first + r) * ORB + l, total[r])
        return carry

    lax.fori_loop(0, ORB // depth, body, 0)


def chunk_swap():
    distance = lane_iota((LANES, LANES)) - row_iota((LANES, LANES))
    group = row_iota((LANES, LANES)) // ROWS
    rows = []
    for a in range(GROUPS):
        row = [((distance == ROWS * (a - b)) & (group == b)).astype(BF16) for b in range(GROUPS)]
        rows.append(jnp.concatenate(row, axis=1))
    return jnp.concatenate(rows, axis=0)


def band(offsets, w_emit, w_absorb, odd, end):
    shape = (ROWS, LANES)
    distance = lane_iota(shape) % ROWS - row_iota(shape)
    before = jnp.zeros(shape, F32)
    here = jnp.zeros(shape, F32)
    after = jnp.zeros(shape, F32)
    for w in range(FREQS):
        off, emit, absorb = offsets[w], w_emit[w], w_absorb[w]
        before = before + jnp.where(distance + ROWS == off, emit, 0.0)
        here = here + jnp.where(distance == off, emit, 0.0) + jnp.where(-distance == off, absorb, 0.0)
        after = after + jnp.where(ROWS - distance == off, absorb, 0.0)
    apart = jnp.where(end, 0.0, jnp.where(odd, after, before))
    beside = jnp.where(odd, before, after)
    group = lane_iota(shape) // ROWS
    parts = []
    for block in (apart, here, beside):
        parts += [jnp.where(group == h, block, 0.0) for h in range(GROUPS)]
    return jnp.concatenate(parts, axis=0).astype(BF16)


def atom_order(first_hot, second_hot):
    in_first = jnp.max(first_hot, axis=1, keepdims=True)
    edge = jnp.maximum(in_first, jnp.max(second_hot, axis=1, keepdims=True))
    shape = (ATOMS, ATOMS)
    earlier = jnp.sum(jnp.where(row_iota(shape) < lane_iota(shape), edge, 0.0), axis=0, keepdims=True)
    itself = row_iota(shape) == lane_iota(shape)
    in_edge = jnp.sum(jnp.where(itself, edge, 0.0), axis=0, keepdims=True)
    in_first = jnp.sum(jnp.where(itself, in_first, 0.0), axis=0, keepdims=True)
    place = jnp.where(in_edge > 0.5, -1.0, lane_iota((1, ATOMS)).astype(F32) - earlier)
    rest = (row_iota((REST, ATOMS)).astype(F32) == place).astype(BF16)
    eye = identity(EDGE)
    first = flip(eye, first_hot.astype(BF16))
    second = flip(eye, second_hot.astype(BF16))
    order = jnp.concatenate([first.astype(BF16), second.astype(BF16), rest], axis=0)
    once = jnp.concatenate([first.astype(BF16), (second * (1.0 - in_first)).astype(BF16), rest], axis=0)
    return order, once


def mixing(neighbours, coupling, order, odd, lowest, highest):
    names = row_iota((ATOMS + 2 * EDGE, ATOMS))
    weights = jnp.zeros((ATOMS + 2 * EDGE, ATOMS), F32)
    for k in range(NBRS):
        weights = weights + jnp.where(names == neighbours[k : k + 1, :], coupling[k : k + 1, :], 0.0)
    low = jnp.where(lowest, 0.0, weights[ATOMS : ATOMS + EDGE])
    high = jnp.where(highest, 0.0, weights[ATOMS + EDGE :])
    edges = [jnp.where(odd, low, high), jnp.where(odd, high, low)]
    weights = jnp.concatenate([weights[:ATOMS]] + edges, axis=0)
    coarse = weights.astype(BF16)
    fine = (weights - coarse.astype(F32)).astype(BF16)
    own = [matmul(order, part[:ATOMS]).astype(BF16) for part in (coarse, fine)]
    edge = [part[ATOMS:] for part in (coarse, fine)]
    return [flip(identity(ATOMS), jnp.concatenate(rows, axis=0)).astype(BF16) for rows in (own, edge)]


def lesser_kernel(
    green, sigma_in, down_list, up_list, green_t, sigma_t, near, far, once, swapper,
    send_down, send_up, green_here, sigma_here, result, grouped, green_semaphores, sigma_semaphores, small_semaphores,
):
    copies = []
    fetched = []
    for n, (source, target) in enumerate(((down_list, send_down), (up_list, send_up))):
        copy = pltpu.make_async_copy(source, target, small_semaphores.at[n])
        copy.start()
        fetched.append(copy)
    moves = ((green, green_here, green_semaphores), (sigma_in, sigma_here, sigma_semaphores))
    for g in range(2):
        copies.append([move_half(source, target, semaphores, g) for source, target, semaphores in moves])
    swapper[...] = chunk_swap()
    for copy in fetched:
        copy.wait()
    below = lax.axis_index("slab") % 2 == 1
    down_hot = (row_iota((ATOMS, EDGE)) == send_down[...]).astype(F32)
    up_hot = (row_iota((ATOMS, EDGE)) == send_up[...]).astype(F32)
    order, once[...] = atom_order(jnp.where(below, down_hot, up_hot), jnp.where(below, up_hot, down_hot))
    for g in range(2):
        for started, source, target in zip(copies[g], (green_here, sigma_here), (green_t, sigma_t)):
            for copy in started:
                copy.wait()
            to_batch_lanes(source, target, g)

        def store(p, value):
            result[p, 8 * g : 8 * g + 8, :] = value

        sandwich_half(green_t, sigma_t, g, store)
    for base in range(0, QUADS, BATCH):
        columns = []
        for j in range(GROUPS):
            columns.append(jnp.concatenate(
                [result[GROUPS * q + j].astype(BF16) for q in range(base, base + BATCH)], axis=0
            ))
        moved = matmul(jnp.concatenate(columns, axis=1), swapper[...]).astype(BF16)
        for i in range(BATCH):
            for h in range(GROUPS):
                grouped[h * NEAR : (h + 1) * NEAR, (base + i) * LANES : (base + i + 1) * LANES] = moved[
                    i * NEAR : (i + 1) * NEAR, h * LANES : (h + 1) * LANES
                ]
    for t in range(WIDTH // WIDE):
        columns = slice(t * WIDE, (t + 1) * WIDE)
        ordered = matmul(order, grouped[:, columns]).astype(BF16)
        near[:, columns] = ordered[: 2 * EDGE]
        far[:, columns] = ordered[2 * EDGE :]


def stack(source, base):
    return jnp.concatenate([source[:, q * LANES : (q + 1) * LANES] for q in range(base, base + BATCH)], axis=0)


def here_kernel(
    offset_list, emit_list, absorb_list, neighbour_list, coupling_list, once, near, near_beside,
    matrix, own_weights, edge_weights, partial, offsets, w_emit, w_absorb, neighbours, coupling, semaphores,
):
    sources = (offset_list, emit_list, absorb_list, neighbour_list, coupling_list)
    targets = (offsets, w_emit, w_absorb, neighbours, coupling)
    copies = []
    for n, (source, target) in enumerate(zip(sources, targets)):
        copy = pltpu.make_async_copy(source, target, semaphores.at[n])
        copy.start()
        copies.append(copy)
    for copy in copies:
        copy.wait()
    slab, energy = lax.axis_index("slab"), lax.axis_index("energy")
    lowest, highest = slab == 0, slab == lax.axis_size("slab") - 1
    end_energy = (energy == 0) | (energy == lax.axis_size("energy") - 1)
    own_weights[...], edge_weights[...] = mixing(neighbours, coupling, once[...], slab % 2 == 1, lowest, highest)
    matrix[...] = band(offsets, w_emit, w_absorb, energy % 2 == 1, end_energy)
    for base in range(0, QUADS, BATCH):
        lhs = jnp.concatenate([stack(near, base), stack(near_beside, base)], axis=1)
        total = matmul(lhs, matrix[LANES:, :])
        for i in range(BATCH):
            column = (base + i) * LANES
            partial[:, column : column + LANES] = total[i * 2 * EDGE : (i + 1) * 2 * EDGE]


def near_kernel(matrix, near_apart, partial, first, second):
    for base in range(0, QUADS, BATCH):
        total = matmul(stack(near_apart, base), matrix[:LANES, :])
        for i in range(BATCH):
            columns = slice((base + i) * LANES, (base + i + 1) * LANES)
            whole = (partial[:, columns] + total[i * 2 * EDGE : (i + 1) * 2 * EDGE]).astype(BF16)
            first[:, columns] = whole[:EDGE]
            second[:, columns] = whole[EDGE:]


def far_kernel(matrix, weights, first, second, far_apart, far, far_beside, mixed, target):
    for base in range(0, QUADS, BATCH):
        lhs = jnp.concatenate([stack(source, base) for source in (far_apart, far, far_beside)], axis=1)
        total = matmul(lhs, matrix[...]).astype(BF16)
        for i in range(BATCH):
            column = (base + i) * LANES
            target[:, column : column + LANES] = total[i * REST : (i + 1) * REST]
    for t in range(WIDTH // WIDE):
        columns = slice(t * WIDE, (t + 1) * WIDE)
        listed = [first[:, columns], second[:, columns], target[:, columns]]
        mixed[:, columns] = matmul(weights[...], jnp.concatenate(listed + listed, axis=0))


def final_kernel(
    weights, swapper, own, first, second, green_t, sigma_t, sigma_ph, g_less,
    flat, flat_less, middle, sigma_here, less_here, semaphores, less_semaphores,
):
    for base in range(0, QUADS, LAST):
        parts = []
        for t in range(base * LANES // WIDE, (base + LAST) * LANES // WIDE):
            columns = slice(t * WIDE, (t + 1) * WIDE)
            listed = [first[:, columns], second[:, columns]]
            edges = matmul(weights[...], jnp.concatenate(listed + listed, axis=0))
            parts.append((own[:, columns] + edges).astype(BF16))
        mixed = jnp.concatenate(parts, axis=1)
        columns = []
        for h in range(GROUPS):
            columns.append(jnp.concatenate(
                [mixed[h * NEAR : (h + 1) * NEAR, i * LANES : (i + 1) * LANES] for i in range(LAST)], axis=0
            ))
        moved = matmul(jnp.concatenate(columns, axis=1), swapper[...])
        for i in range(LAST):
            for j in range(GROUPS):
                part = moved[i * NEAR : (i + 1) * NEAR, j * LANES : (j + 1) * LANES]
                for g in range(2):
                    rows = atom_rows(GROUPS * (base + i) + j, g)
                    flat[rows, :] = part[8 * g : 8 * g + 8]
                    middle[rows, :] = sigma_t[rows, :] + part[8 * g : 8 * g + 8]
    copies = []
    to_energy_rows(flat, sigma_here, 0)
    copies += move_half(sigma_here, sigma_ph, semaphores, 0)

    for g in range(2):
        def store(p, value):
            flat_less[atom_rows(p, g), :] = value

        sandwich_half(green_t, middle, g, store)
        to_energy_rows(flat_less, less_here, g)
        copies += move_half(less_here, g_less, less_semaphores, g)
        if g == 0:
            to_energy_rows(flat, sigma_here, 1)
            copies += move_half(sigma_here, sigma_ph, semaphores, 1)
    for copy in copies:
        copy.wait()


def vmem(count):
    return [pl.BlockSpec(memory_space=pltpu.VMEM)] * count


def anywhere(count):
    return [pl.BlockSpec(memory_space=pl.ANY)] * count


PARAMS = pltpu.CompilerParams(vmem_limit_bytes=44 * 1024 * 1024)


def pair_up(block, partner):
    energies, slabs = lax.axis_size("energy"), lax.axis_size("slab")
    pairs = []
    for energy in range(energies):
        for slab in range(slabs):
            other_energy, other_slab = partner(energy, slab, energies, slabs)
            pairs.append((energy * slabs + slab, other_energy * slabs + other_slab))
    return lax.ppermute(block, ("energy", "slab"), pairs)


def beside(energy, slab, energies, slabs):
    return energy ^ 1, slab


def apart(energy, slab, energies, slabs):
    other = ((energy + 1) ^ 1) - 1
    if 0 <= other < energies:
        return other, slab
    return energy, slab ^ 1


def slab_step(energy, slab, slabs, step, aside):
    if 0 <= slab + step < slabs:
        return energy, slab + step
    return energy ^ aside, slab


def first_slab(energy, slab, energies, slabs):
    return slab_step(energy, slab, slabs, 1 if slab % 2 == 0 else -1, 1)


def second_slab(energy, slab, energies, slabs):
    return slab_step(energy, slab, slabs, -1 if slab % 2 == 0 else 1, 1)


def shape_of(*shape, kind=BF16):
    return jax.ShapeDtypeStruct(shape, kind)


def in_hbm(arrays):
    return [pltpu.with_memory_space_constraint(array, pltpu.HBM) for array in arrays]


def on_device(green, sigma_in, neighbours, coupling, send_down, send_up, offsets, w_emit, w_absorb):
    tall = shape_of(NEAR * PITCH, LANES, kind=F32)
    half = shape_of(2 * EDGE, WIDTH)
    edge = shape_of(EDGE, WIDTH)
    green_t, sigma_t, near, far, once, swapper = pl.pallas_call(
        lesser_kernel,
        out_shape=(tall, tall, half, shape_of(REST, WIDTH), shape_of(NAMED, ATOMS), shape_of(WIDE, WIDE)),
        in_specs=anywhere(4),
        out_specs=tuple(vmem(6)),
        scratch_shapes=[
            pltpu.VMEM((1, EDGE), jnp.int32),
            pltpu.VMEM((1, EDGE), jnp.int32),
            pltpu.VMEM((ROWS, ATOMS * PAIRS), BF16),
            pltpu.VMEM((ROWS, ATOMS * PAIRS), BF16),
            pltpu.VMEM((PAIRS, NEAR, LANES), F32),
            pltpu.VMEM((ATOMS, WIDTH), BF16),
            pltpu.SemaphoreType.DMA((2 * GROUPS,)),
            pltpu.SemaphoreType.DMA((2 * GROUPS,)),
            pltpu.SemaphoreType.DMA((2,)),
        ],
        compiler_params=PARAMS,
    )(*in_hbm((green, sigma_in, send_down, send_up)))
    near_apart = pair_up(near, apart)
    near_beside = pair_up(near, beside)
    far_apart = pair_up(far, apart)
    far_beside = pair_up(far, beside)
    matrix, own_weights, edge_weights, partial = pl.pallas_call(
        here_kernel,
        out_shape=(
            shape_of(3 * LANES, LANES), shape_of(ATOMS, 2 * NAMED), shape_of(ATOMS, 4 * EDGE),
            shape_of(2 * EDGE, WIDTH, kind=F32),
        ),
        in_specs=anywhere(5) + vmem(3),
        out_specs=tuple(vmem(4)),
        scratch_shapes=[
            pltpu.SMEM((FREQS,), jnp.int32),
            pltpu.SMEM((FREQS,), F32),
            pltpu.SMEM((FREQS,), F32),
            pltpu.VMEM((NBRS, ATOMS), jnp.int32),
            pltpu.VMEM((NBRS, ATOMS), F32),
            pltpu.SemaphoreType.DMA((5,)),
        ],
        compiler_params=PARAMS,
    )(*in_hbm((offsets, w_emit, w_absorb, neighbours.T, coupling.T)), once, near, near_beside)
    first, second = pl.pallas_call(
        near_kernel,
        out_shape=(edge, edge),
        in_specs=vmem(3),
        out_specs=tuple(vmem(2)),
        compiler_params=PARAMS,
    )(matrix, near_apart, partial)
    own = pl.pallas_call(
        far_kernel,
        out_shape=shape_of(ATOMS, WIDTH, kind=F32),
        in_specs=vmem(7),
        out_specs=vmem(1)[0],
        scratch_shapes=[pltpu.VMEM((REST, WIDTH), BF16)],
        compiler_params=PARAMS,
    )(matrix, own_weights, first, second, far_apart, far, far_beside)
    first = pair_up(first, first_slab)
    second = pair_up(second, second_slab)
    flat = shape_of(ROWS, ATOMS * PAIRS)
    return pl.pallas_call(
        final_kernel,
        out_shape=(flat, flat),
        in_specs=vmem(7),
        out_specs=tuple(anywhere(2)),
        scratch_shapes=[
            pltpu.VMEM((NEAR * PITCH, LANES), F32),
            pltpu.VMEM((NEAR * PITCH, LANES), F32),
            pltpu.VMEM((NEAR * PITCH, LANES), F32),
            pltpu.VMEM((ROWS, ATOMS * PAIRS), BF16),
            pltpu.VMEM((ROWS, ATOMS * PAIRS), BF16),
            pltpu.SemaphoreType.DMA((2 * GROUPS,)),
            pltpu.SemaphoreType.DMA((2 * GROUPS,)),
        ],
        compiler_params=PARAMS,
    )(edge_weights, swapper, own, first, second, green_t, sigma_t)


def solution(mesh):
    split = P("energy", "slab")
    by_slab = P("slab", None)
    return jax.shard_map(
        on_device,
        mesh=mesh,
        in_specs=(split, split, by_slab, by_slab, by_slab, by_slab, P(), P(), P()),
        out_specs=(split, split),
        check_vma=False,
    )
```

```python
import jax
import jax.numpy as jnp
from jax import lax
from jax.experimental import pallas as pl
from jax.experimental.pallas import tpu as pltpu
from jax.sharding import PartitionSpec as P

ORB = 12
PAIRS = 144
NBRS = 8
FREQS = 16
LANES = 128
GROUPS = 4
ROWS = 32
ATOMS = 64
EDGE = 16
REST = ATOMS - EDGE
NAMED = ATOMS + EDGE
NEAR = 16
SPAN = NEAR * PAIRS
PITCH = PAIRS + 1
TALL = 8 * ((NEAR + 1) * PITCH // 8 + 1)
TILES = SPAN // LANES
QUADS = PAIRS // GROUPS
WIDTH = PAIRS * ROWS
WIDE = 512
BATCH = 12
LAST = 36
F32 = jnp.float32
BF16 = jnp.bfloat16


def lane_iota(shape):
    return lax.broadcasted_iota(jnp.int32, shape, len(shape) - 1)


def row_iota(shape):
    return lax.broadcasted_iota(jnp.int32, shape, len(shape) - 2)


def identity(size):
    return (lane_iota((size, size)) == row_iota((size, size))).astype(BF16)


def matmul(lhs, rhs):
    return jnp.dot(lhs, rhs, preferred_element_type=F32)


def matmul_first(lhs, rhs):
    return lax.dot_general(lhs, rhs, (((0,), (0,)), ((), ())), preferred_element_type=F32)


def flip(eye, tile):
    return lax.dot_general(eye, tile, (((1,), (1,)), ((), ())), preferred_element_type=F32)


def pieces(t):
    row, stop = t * LANES, (t + 1) * LANES
    while row < stop:
        atom = row // PAIRS
        size = min(stop, (atom + 1) * PAIRS) - row
        yield row - t * LANES, row + atom * (PITCH - PAIRS), size
        row += size


def atom_rows(p, g):
    return pl.ds(8 * g * PITCH + p, 8, stride=PITCH)


def to_batch_lanes(source, target, half):
    for t in range(half * TILES // 2, (half + 1) * TILES // 2):
        columns = [source[:, h * SPAN + t * LANES : h * SPAN + (t + 1) * LANES] for h in range(GROUPS)]
        turned = jnp.concatenate(columns, axis=0).T.astype(F32)
        for start, row, size in pieces(t):
            target[row : row + size, :] = turned[start : start + size]


def to_energy_rows(flat, target, half):
    for t in range(half * TILES // 2, (half + 1) * TILES // 2):
        rows = [flat[row : row + size, :].astype(BF16) for _, row, size in pieces(t)]
        turned = jnp.concatenate(rows, axis=0).T
        for h in range(GROUPS):
            column = h * SPAN + t * LANES
            target[:, column : column + LANES] = turned[h * ROWS : (h + 1) * ROWS]


def move_half(source, target, semaphores, half):
    copies = []
    for h in range(GROUPS):
        columns = pl.ds(h * SPAN + half * SPAN // 2, SPAN // 2)
        copy = pltpu.make_async_copy(source.at[:, columns], target.at[:, columns], semaphores.at[half * GROUPS + h])
        copy.start()
        copies.append(copy)
    return copies


def sandwich_half(left, middle, g, store):
    depth = 3
    def body(step, carry):
        first = step * depth
        product = [[None] * ORB for _ in range(depth)]
        for j in range(ORB):
            lhs = [left[atom_rows((first + r) * ORB + j, g), :] for r in range(depth)]
            for k in range(ORB):
                rhs = middle[atom_rows(j * ORB + k, g), :]
                for r in range(depth):
                    term = lhs[r] * rhs
                    product[r][k] = term if j == 0 else product[r][k] + term
        for l in range(ORB):
            total = [None] * depth
            for k in range(ORB):
                rhs = left[atom_rows(l * ORB + k, g), :]
                for r in range(depth):
                    term = product[r][k] * rhs
                    total[r] = term if k == 0 else total[r] + term
            for r in range(depth):
                store((first + r) * ORB + l, total[r])
        return carry

    lax.fori_loop(0, ORB // depth, body, 0)


def chunk_swap():
    distance = lane_iota((LANES, LANES)) - row_iota((LANES, LANES))
    group = row_iota((LANES, LANES)) // ROWS
    rows = []
    for a in range(GROUPS):
        row = [((distance == ROWS * (a - b)) & (group == b)).astype(BF16) for b in range(GROUPS)]
        rows.append(jnp.concatenate(row, axis=1))
    return jnp.concatenate(rows, axis=0)


def band(offsets, w_emit, w_absorb, odd, end):
    shape = (ROWS, LANES)
    distance = lane_iota(shape) % ROWS - row_iota(shape)
    before = jnp.zeros(shape, F32)
    here = jnp.zeros(shape, F32)
    after = jnp.zeros(shape, F32)
    for w in range(FREQS):
        off, emit, absorb = offsets[w], w_emit[w], w_absorb[w]
        before = before + jnp.where(distance + ROWS == off, emit, 0.0)
        here = here + jnp.where(distance == off, emit, 0.0) + jnp.where(-distance == off, absorb, 0.0)
        after = after + jnp.where(ROWS - distance == off, absorb, 0.0)
    apart = jnp.where(end, 0.0, jnp.where(odd, after, before))
    beside = jnp.where(odd, before, after)
    group = lane_iota(shape) // ROWS
    parts = []
    for block in (apart, here, beside):
        parts += [jnp.where(group == h, block, 0.0) for h in range(GROUPS)]
    return jnp.concatenate(parts, axis=0).astype(BF16)


def atom_order(first_hot, second_hot):
    in_first = jnp.max(first_hot, axis=1, keepdims=True)
    edge = jnp.maximum(in_first, jnp.max(second_hot, axis=1, keepdims=True))
    shape = (ATOMS, ATOMS)
    earlier = jnp.sum(jnp.where(row_iota(shape) < lane_iota(shape), edge, 0.0), axis=0, keepdims=True)
    itself = row_iota(shape) == lane_iota(shape)
    in_edge = jnp.sum(jnp.where(itself, edge, 0.0), axis=0, keepdims=True)
    in_first = jnp.sum(jnp.where(itself, in_first, 0.0), axis=0, keepdims=True)
    place = jnp.where(in_edge > 0.5, -1.0, lane_iota((1, ATOMS)).astype(F32) - earlier)
    rest = (row_iota((REST, ATOMS)).astype(F32) == place).astype(BF16)
    eye = identity(EDGE)
    first = flip(eye, first_hot.astype(BF16))
    second = flip(eye, second_hot.astype(BF16))
    order = jnp.concatenate([first.astype(BF16), second.astype(BF16), rest], axis=0)
    once = jnp.concatenate([first.astype(BF16), (second * (1.0 - in_first)).astype(BF16), rest], axis=0)
    return order, once


def mixing(neighbours, coupling, order, odd, lowest, highest):
    names = row_iota((ATOMS + 2 * EDGE, ATOMS))
    weights = jnp.zeros((ATOMS + 2 * EDGE, ATOMS), F32)
    for k in range(NBRS):
        weights = weights + jnp.where(names == neighbours[k : k + 1, :], coupling[k : k + 1, :], 0.0)
    low = jnp.where(lowest, 0.0, weights[ATOMS : ATOMS + EDGE])
    high = jnp.where(highest, 0.0, weights[ATOMS + EDGE :])
    edges = [jnp.where(odd, low, high), jnp.where(odd, high, low)]
    weights = jnp.concatenate([weights[:ATOMS]] + edges, axis=0)
    coarse = weights.astype(BF16)
    fine = (weights - coarse.astype(F32)).astype(BF16)
    own = [matmul(order, part[:ATOMS]).astype(BF16) for part in (coarse, fine)]
    edge = [part[ATOMS:] for part in (coarse, fine)]
    return [flip(identity(ATOMS), jnp.concatenate(rows, axis=0)).astype(BF16) for rows in (own, edge)]


def lesser_kernel(
    green, sigma_in, down_list, up_list, green_t, sigma_t, near, far, once, swapper,
    send_down, send_up, green_here, sigma_here, result, grouped, green_semaphores, sigma_semaphores, small_semaphores,
):
    copies = []
    fetched = []
    for n, (source, target) in enumerate(((down_list, send_down), (up_list, send_up))):
        copy = pltpu.make_async_copy(source, target, small_semaphores.at[n])
        copy.start()
        fetched.append(copy)
    moves = ((green, green_here, green_semaphores), (sigma_in, sigma_here, sigma_semaphores))
    for g in range(2):
        copies.append([move_half(source, target, semaphores, g) for source, target, semaphores in moves])
    swapper[...] = chunk_swap()
    for copy in fetched:
        copy.wait()
    below = lax.axis_index("slab") % 2 == 1
    down_hot = (row_iota((ATOMS, EDGE)) == send_down[...]).astype(F32)
    up_hot = (row_iota((ATOMS, EDGE)) == send_up[...]).astype(F32)
    order, once[...] = atom_order(jnp.where(below, down_hot, up_hot), jnp.where(below, up_hot, down_hot))
    for g in range(2):
        for started, source, target in zip(copies[g], (green_here, sigma_here), (green_t, sigma_t)):
            for copy in started:
                copy.wait()
            to_batch_lanes(source, target, g)

        def store(p, value):
            result[p, 8 * g : 8 * g + 8, :] = value

        sandwich_half(green_t, sigma_t, g, store)
    for base in range(0, QUADS, BATCH):
        columns = []
        for j in range(GROUPS):
            columns.append(jnp.concatenate(
                [result[GROUPS * q + j].astype(BF16) for q in range(base, base + BATCH)], axis=0
            ))
        moved = matmul(jnp.concatenate(columns, axis=1), swapper[...]).astype(BF16)
        for i in range(BATCH):
            for h in range(GROUPS):
                grouped[h * NEAR : (h + 1) * NEAR, (base + i) * LANES : (base + i + 1) * LANES] = moved[
                    i * NEAR : (i + 1) * NEAR, h * LANES : (h + 1) * LANES
                ]
    for t in range(WIDTH // WIDE):
        columns = slice(t * WIDE, (t + 1) * WIDE)
        ordered = matmul(order, grouped[:, columns]).astype(BF16)
        near[:, columns] = ordered[: 2 * EDGE]
        far[:, columns] = ordered[2 * EDGE :]


def stack(source, base):
    return jnp.concatenate([source[:, q * LANES : (q + 1) * LANES] for q in range(base, base + BATCH)], axis=0)


def here_kernel(
    offset_list, emit_list, absorb_list, neighbour_list, coupling_list, once, near, near_beside,
    matrix, own_weights, edge_weights, partial, offsets, w_emit, w_absorb, neighbours, coupling, semaphores,
):
    sources = (offset_list, emit_list, absorb_list, neighbour_list, coupling_list)
    targets = (offsets, w_emit, w_absorb, neighbours, coupling)
    copies = []
    for n, (source, target) in enumerate(zip(sources, targets)):
        copy = pltpu.make_async_copy(source, target, semaphores.at[n])
        copy.start()
        copies.append(copy)
    for copy in copies:
        copy.wait()
    slab, energy = lax.axis_index("slab"), lax.axis_index("energy")
    lowest, highest = slab == 0, slab == lax.axis_size("slab") - 1
    end_energy = (energy == 0) | (energy == lax.axis_size("energy") - 1)
    own_weights[...], edge_weights[...] = mixing(neighbours, coupling, once[...], slab % 2 == 1, lowest, highest)
    matrix[...] = band(offsets, w_emit, w_absorb, energy % 2 == 1, end_energy)
    for base in range(0, QUADS, BATCH):
        lhs = jnp.concatenate([stack(near, base), stack(near_beside, base)], axis=1)
        total = matmul(lhs, matrix[LANES:, :])
        for i in range(BATCH):
            column = (base + i) * LANES
            partial[:, column : column + LANES] = total[i * 2 * EDGE : (i + 1) * 2 * EDGE]


def near_kernel(matrix, near_apart, partial, first, second):
    for base in range(0, QUADS, BATCH):
        total = matmul(stack(near_apart, base), matrix[:LANES, :])
        for i in range(BATCH):
            columns = slice((base + i) * LANES, (base + i + 1) * LANES)
            whole = (partial[:, columns] + total[i * 2 * EDGE : (i + 1) * 2 * EDGE]).astype(BF16)
            first[:, columns] = whole[:EDGE]
            second[:, columns] = whole[EDGE:]


def far_kernel(matrix, weights, first, second, far_apart, far, far_beside, mixed, target):
    for base in range(0, QUADS, BATCH):
        lhs = jnp.concatenate([stack(source, base) for source in (far_apart, far, far_beside)], axis=1)
        total = matmul(lhs, matrix[...]).astype(BF16)
        for i in range(BATCH):
            column = (base + i) * LANES
            target[:, column : column + LANES] = total[i * REST : (i + 1) * REST]
    for t in range(WIDTH // WIDE):
        columns = slice(t * WIDE, (t + 1) * WIDE)
        listed = [first[:, columns], second[:, columns], target[:, columns]]
        mixed[:, columns] = matmul(weights[...], jnp.concatenate(listed + listed, axis=0))


def final_kernel(
    weights, swapper, own, first, second, green_t, sigma_t, sigma_ph, g_less,
    flat, flat_less, middle, sigma_here, less_here, semaphores, less_semaphores,
):
    for base in range(0, QUADS, LAST):
        parts = []
        for t in range(base * LANES // WIDE, (base + LAST) * LANES // WIDE):
            columns = slice(t * WIDE, (t + 1) * WIDE)
            listed = [first[:, columns], second[:, columns]]
            edges = matmul(weights[...], jnp.concatenate(listed + listed, axis=0))
            parts.append((own[:, columns] + edges).astype(BF16))
        mixed = jnp.concatenate(parts, axis=1)
        columns = []
        for h in range(GROUPS):
            columns.append(jnp.concatenate(
                [mixed[h * NEAR : (h + 1) * NEAR, i * LANES : (i + 1) * LANES] for i in range(LAST)], axis=0
            ))
        moved = matmul(jnp.concatenate(columns, axis=1), swapper[...])
        for i in range(LAST):
            for j in range(GROUPS):
                part = moved[i * NEAR : (i + 1) * NEAR, j * LANES : (j + 1) * LANES]
                for g in range(2):
                    rows = atom_rows(GROUPS * (base + i) + j, g)
                    flat[rows, :] = part[8 * g : 8 * g + 8]
                    middle[rows, :] = sigma_t[rows, :] + part[8 * g : 8 * g + 8]
    copies = []
    to_energy_rows(flat, sigma_here, 0)
    copies += move_half(sigma_here, sigma_ph, semaphores, 0)

    for g in range(2):
        def store(p, value):
            flat_less[atom_rows(p, g), :] = value

        sandwich_half(green_t, middle, g, store)
        to_energy_rows(flat_less, less_here, g)
        copies += move_half(less_here, g_less, less_semaphores, g)
        if g == 0:
            to_energy_rows(flat, sigma_here, 1)
            copies += move_half(sigma_here, sigma_ph, semaphores, 1)
    for copy in copies:
        copy.wait()


def vmem(count):
    return [pl.BlockSpec(memory_space=pltpu.VMEM)] * count


def anywhere(count):
    return [pl.BlockSpec(memory_space=pl.ANY)] * count


PARAMS = pltpu.CompilerParams(vmem_limit_bytes=44 * 1024 * 1024)


def pair_up(block, partner):
    energies, slabs = lax.axis_size("energy"), lax.axis_size("slab")
    pairs = []
    for energy in range(energies):
        for slab in range(slabs):
            other_energy, other_slab = partner(energy, slab, energies, slabs)
            pairs.append((energy * slabs + slab, other_energy * slabs + other_slab))
    return lax.ppermute(block, ("energy", "slab"), pairs)


def beside(energy, slab, energies, slabs):
    return energy ^ 1, slab


def apart(energy, slab, energies, slabs):
    other = ((energy + 1) ^ 1) - 1
    if 0 <= other < energies:
        return other, slab
    return energy, slab ^ 1


def slab_step(energy, slab, slabs, step, aside):
    if 0 <= slab + step < slabs:
        return energy, slab + step
    return energy ^ aside, slab


def first_slab(energy, slab, energies, slabs):
    return slab_step(energy, slab, slabs, 1 if slab % 2 == 0 else -1, 1)


def second_slab(energy, slab, energies, slabs):
    return slab_step(energy, slab, slabs, -1 if slab % 2 == 0 else 1, 1)


def shape_of(*shape, kind=BF16):
    return jax.ShapeDtypeStruct(shape, kind)


def in_hbm(arrays):
    return [pltpu.with_memory_space_constraint(array, pltpu.HBM) for array in arrays]


def on_device(green, sigma_in, neighbours, coupling, send_down, send_up, offsets, w_emit, w_absorb):
    tall = shape_of(TALL, LANES, kind=F32)
    half = shape_of(2 * EDGE, WIDTH)
    edge = shape_of(EDGE, WIDTH)
    green_t, sigma_t, near, far, once, swapper = pl.pallas_call(
        lesser_kernel,
        out_shape=(tall, tall, half, shape_of(REST, WIDTH), shape_of(NAMED, ATOMS), shape_of(WIDE, WIDE)),
        in_specs=anywhere(4),
        out_specs=tuple(vmem(6)),
        scratch_shapes=[
            pltpu.VMEM((1, EDGE), jnp.int32),
            pltpu.VMEM((1, EDGE), jnp.int32),
            pltpu.VMEM((ROWS, ATOMS * PAIRS), BF16),
            pltpu.VMEM((ROWS, ATOMS * PAIRS), BF16),
            pltpu.VMEM((PAIRS, NEAR, LANES), F32),
            pltpu.VMEM((ATOMS, WIDTH), BF16),
            pltpu.SemaphoreType.DMA((2 * GROUPS,)),
            pltpu.SemaphoreType.DMA((2 * GROUPS,)),
            pltpu.SemaphoreType.DMA((2,)),
        ],
        compiler_params=PARAMS,
    )(*in_hbm((green, sigma_in, send_down, send_up)))
    near_apart = pair_up(near, apart)
    near_beside = pair_up(near, beside)
    far_apart = pair_up(far, apart)
    far_beside = pair_up(far, beside)
    matrix, own_weights, edge_weights, partial = pl.pallas_call(
        here_kernel,
        out_shape=(
            shape_of(3 * LANES, LANES), shape_of(ATOMS, 2 * NAMED), shape_of(ATOMS, 4 * EDGE),
            shape_of(2 * EDGE, WIDTH, kind=F32),
        ),
        in_specs=anywhere(5) + vmem(3),
        out_specs=tuple(vmem(4)),
        scratch_shapes=[
            pltpu.SMEM((FREQS,), jnp.int32),
            pltpu.SMEM((FREQS,), F32),
            pltpu.SMEM((FREQS,), F32),
            pltpu.VMEM((NBRS, ATOMS), jnp.int32),
            pltpu.VMEM((NBRS, ATOMS), F32),
            pltpu.SemaphoreType.DMA((5,)),
        ],
        compiler_params=PARAMS,
    )(*in_hbm((offsets, w_emit, w_absorb, neighbours.T, coupling.T)), once, near, near_beside)
    first, second = pl.pallas_call(
        near_kernel,
        out_shape=(edge, edge),
        in_specs=vmem(3),
        out_specs=tuple(vmem(2)),
        compiler_params=PARAMS,
    )(matrix, near_apart, partial)
    own = pl.pallas_call(
        far_kernel,
        out_shape=shape_of(ATOMS, WIDTH, kind=F32),
        in_specs=vmem(7),
        out_specs=vmem(1)[0],
        scratch_shapes=[pltpu.VMEM((REST, WIDTH), BF16)],
        compiler_params=PARAMS,
    )(matrix, own_weights, first, second, far_apart, far, far_beside)
    first = pair_up(first, first_slab)
    second = pair_up(second, second_slab)
    flat = shape_of(ROWS, ATOMS * PAIRS)
    return pl.pallas_call(
        final_kernel,
        out_shape=(flat, flat),
        in_specs=vmem(7),
        out_specs=tuple(anywhere(2)),
        scratch_shapes=[
            pltpu.VMEM((TALL, LANES), F32),
            pltpu.VMEM((TALL, LANES), F32),
            pltpu.VMEM((TALL, LANES), F32),
            pltpu.VMEM((ROWS, ATOMS * PAIRS), BF16),
            pltpu.VMEM((ROWS, ATOMS * PAIRS), BF16),
            pltpu.SemaphoreType.DMA((2 * GROUPS,)),
            pltpu.SemaphoreType.DMA((2 * GROUPS,)),
        ],
        compiler_params=PARAMS,
    )(edge_weights, swapper, own, first, second, green_t, sigma_t)


def solution(mesh):
    split = P("energy", "slab")
    by_slab = P("slab", None)
    return jax.shard_map(
        on_device,
        mesh=mesh,
        in_specs=(split, split, by_slab, by_slab, by_slab, by_slab, P(), P(), P()),
        out_specs=(split, split),
        check_vma=False,
    )
```
